128 devices in a mesh: seq: 4 (over y), slide: 32 (over x, z, core).
Axes of the slice: x: 4, y: 4, z: 4, core: 2. Of those that a mesh axis runs over, the one named last changes fastest.
Arguments:
- patches: bfloat16 [32, 4096, 768], P('slide', 'seq'), may hold values from -13 to 13
- w_query: bfloat16 [768, 768], replicated
- w_key: bfloat16 [768, 768], replicated
- w_value: bfloat16 [768, 768], replicated, may hold values from -0.21875 to 0.21875
- w_out: bfloat16 [768, 768], replicated, may hold values from -0.21875 to 0.21875
- lengths: int32 [32], P('slide'), may hold values from 512 to 4096, as said below
- cotangent: bfloat16 [32, 4096, 768], P('slide', 'seq'), may hold values from -6 to 6
Outputs:
- attended: bfloat16 [32, 4096, 768], P('slide', 'seq')
- grad_patches: bfloat16 [32, 4096, 768], P('slide', 'seq')
- grad_query: bfloat16 [768, 768], replicated
- grad_key: bfloat16 [768, 768], replicated
- grad_value: bfloat16 [768, 768], replicated
- grad_out: bfloat16 [768, 768], replicated
The draws below stay inside these ranges and needn't reach their ends.
Inputs may be any that keep to these rules, and one draw needn't show every extreme that they name: The first lengths[s] positions of slide s are patches, the rest of its span is padding; some slide fills all 4096 positions.
All inputs are finite; a program needn't handle non-finite values.
Results may differ from the reference program's by a relative error of at most 0.025.
Values may be sent and summed in bfloat16 or wider, within the bound.
A program may use at most 192 MiB of HBM per device.

```python
import math
import jax
import jax.numpy as jnp
from jax import lax

D = 768
ATTENTION_HEADS = 12
SEGMENT = 1024
FAR_DILATION = 4
SPAN = 4096
SLIDES = 32


def shared_basis(key):
    return jnp.clip(jax.random.normal(key, (D, D), jnp.float32), -5.0, 5.0) / math.sqrt(D)


def draw_w_query(key, part):
    common = shared_basis(key)
    key = jax.random.fold_in(key, 2)
    own_part = jnp.clip(jax.random.normal(key, (D, D), jnp.float32), -5.0, 5.0) / math.sqrt(D)
    return (0.8 * common + 0.6 * own_part).astype(jnp.bfloat16)


def draw_w_key(key, part):
    common = shared_basis(key)
    key = jax.random.fold_in(key, 3)
    own_part = jnp.clip(jax.random.normal(key, (D, D), jnp.float32), -5.0, 5.0) / math.sqrt(D)
    return (0.8 * common + 0.6 * own_part).astype(jnp.bfloat16)


def draw_patches(key, part):
    key = jax.random.fold_in(key, 1)
    return jnp.clip(jax.random.normal(key, (SLIDES, SPAN, D), jnp.float32), -6.0, 6.0).astype(jnp.bfloat16)


def draw_lengths(key, part):
    key = jax.random.fold_in(key, 4)
    key_a, key_b = jax.random.split(key)
    drawn = jax.random.randint(key_a, (SLIDES,), SPAN // 8, SPAN + 1)
    fuller = jax.random.randint(key_b, (), 0, SLIDES)
    return jnp.where(jnp.arange(SLIDES) == fuller, SPAN, drawn).astype(jnp.int32)


def steps_of(key, shape, pieces, smallest, largest):
    def one(axis_at, shards_of):
        draws = jax.random.uniform(jax.random.fold_in(jax.random.fold_in(key, 6), axis_at), (shards_of,), jnp.float32, smallest / len(pieces), largest / len(pieces))
        return jnp.repeat(jnp.exp(draws), shape[axis_at] // shards_of).reshape((-1,) + (1,) * (len(shape) - axis_at - 1))

    factor_of = one(*pieces[0])
    for cut in pieces[1:]:
        factor_of = factor_of * one(*cut)
    return factor_of


def gaussian(rng, extent, scale, limit, cuts=(), kind=jnp.bfloat16):
    values = jax.random.normal(rng, extent, jnp.float32) * scale
    if len(cuts) > 0:
        values = steps_of(rng, extent, cuts, -0.22, 0.18) * values
    return jnp.clip(values, min=-limit, max=limit).astype(kind)


def setup_inputs(seed: int = 0) -> dict:
    seeds = jax.random.split(jax.random.key(seed), 8)
    patches = draw_patches(jax.random.fold_in(seeds[7], 71), 0)
    w_query = draw_w_query(jax.random.fold_in(seeds[7], 71), 0)
    w_key = draw_w_key(jax.random.fold_in(seeds[7], 71), 0)
    w_value = gaussian(seeds[3], (D, D), D ** -0.5, 0.21875)
    w_out = gaussian(seeds[4], (D, D), D ** -0.5, 0.21875)
    lengths = draw_lengths(jax.random.fold_in(seeds[7], 71), 0)
    cotangent = gaussian(seeds[6], (SLIDES, SPAN, D), 1.0, 6.0, ((0, 32), (1, 4)))
    return dict(patches=patches, w_query=w_query, w_key=w_key, w_value=w_value, w_out=w_out, lengths=lengths, cotangent=cotangent)


NEGATIVE = -1e+30

def rounded(array):
    return lax.optimization_barrier(array.astype(jnp.bfloat16)).astype(jnp.float32)

def pick_rows(block_span, head_total_count):
    leading_shape = block_span.shape[:-2]
    total_row_count, feature_channel_width = block_span.shape[-2:]
    head_feature_width = feature_channel_width // head_total_count
    memory_layout = block_span.reshape(leading_shape + (total_row_count // FAR_DILATION, FAR_DILATION, head_total_count, head_feature_width))
    chosen_tokens = [memory_layout[..., segment_member % FAR_DILATION, segment_member, :] for segment_member in range(head_total_count)]
    return jnp.stack(chosen_tokens, axis=-2).reshape(leading_shape + (total_row_count // FAR_DILATION, feature_channel_width))

def place_rows(chosen_tokens, head_total_count):
    selected_count, feature_channel_width = chosen_tokens.shape
    head_feature_width = feature_channel_width // head_total_count
    selection_mask = (jnp.arange(FAR_DILATION)[:, None] == (jnp.arange(head_total_count) % FAR_DILATION)[None, :]).astype(chosen_tokens.dtype)
    dilation_spread = chosen_tokens.reshape(selected_count, 1, head_total_count, head_feature_width) * selection_mask[None, :, :, None]
    return dilation_spread.reshape(selected_count * FAR_DILATION, feature_channel_width)

def to_heads(array):
    return array.reshape(array.shape[0], ATTENTION_HEADS, -1).transpose(1, 0, 2)

def from_heads(array):
    return array.transpose(1, 0, 2).reshape(array.shape[1], -1)

def head_pass(operands, positions, length):
    query_rows, key_rows, value_rows, distant_keys, far_values, context_gradient, start_offset = operands
    total_row_count, head_feature_width = query_rows.shape
    selected_count = total_row_count // FAR_DILATION
    segments = total_row_count // SEGMENT
    score_scale_factor = 1.0 / math.sqrt(head_feature_width)
    valid_token_mask = positions < length
    column_active = jnp.arange(FAR_DILATION, dtype=jnp.int32) == start_offset
    distant_positions = jnp.arange(distant_keys.shape[0], dtype=jnp.int32) * FAR_DILATION + start_offset
    query_full = query_rows.astype(jnp.float32)
    full_gradient = context_gradient.astype(jnp.float32)
    fk_full = distant_keys.astype(jnp.float32)
    fv_full = far_values.astype(jnp.float32)
    query_segment = query_full.reshape(segments, SEGMENT, head_feature_width)
    key_segment = key_rows.astype(jnp.float32).reshape(segments, SEGMENT, head_feature_width)
    value_segment = value_rows.astype(jnp.float32).reshape(segments, SEGMENT, head_feature_width)
    segment_gradient = full_gradient.reshape(segments, SEGMENT, head_feature_width)
    local_scores = jnp.einsum('mhr,mtr->mht', query_segment, key_segment) * score_scale_factor
    local_scores = jnp.where(valid_token_mask.reshape(segments, SEGMENT)[:, None, :], local_scores, NEGATIVE)
    query_selected = lax.dynamic_index_in_dim(query_full.reshape(selected_count, FAR_DILATION, head_feature_width), start_offset, 1, keepdims=False)
    selected_gradient = lax.dynamic_index_in_dim(full_gradient.reshape(selected_count, FAR_DILATION, head_feature_width), start_offset, 1, keepdims=False)
    far_scores = jnp.einsum('qd,kd->qk', query_selected, fk_full) * score_scale_factor
    far_scores = jnp.where((distant_positions < length)[None, :], far_scores, NEGATIVE)
    local_maximum = lax.optimization_barrier(jnp.max(local_scores, axis=-1)).reshape(selected_count, FAR_DILATION)
    far_peak = lax.optimization_barrier(jnp.max(far_scores, axis=-1))
    pick_peak = jnp.maximum(lax.dynamic_index_in_dim(local_maximum, start_offset, 1, keepdims=False), far_peak)
    row_peak = jnp.where(column_active[None, :], pick_peak[:, None], local_maximum)
    local_exponent = jnp.exp(local_scores - row_peak.reshape(segments, SEGMENT)[:, :, None])
    distant_exponent = jnp.exp(far_scores - pick_peak[:, None])
    softmax_denominator = lax.optimization_barrier(jnp.sum(local_exponent, axis=-1)).reshape(selected_count, FAR_DILATION) + jnp.where(column_active[None, :], lax.optimization_barrier(jnp.sum(distant_exponent, axis=-1))[:, None], 0.0)
    row_weight_factor = valid_token_mask.astype(jnp.float32).reshape(selected_count, FAR_DILATION) / softmax_denominator
    near_prob = local_exponent * row_weight_factor.reshape(segments, SEGMENT)[:, :, None]
    far_prob = distant_exponent * lax.dynamic_index_in_dim(row_weight_factor, start_offset, 1, keepdims=False)[:, None]
    local_rounded = rounded(near_prob)
    far_round = rounded(far_prob)
    local_output = jnp.einsum('wun,wnj->wuj', local_rounded, value_segment).reshape(selected_count, FAR_DILATION, head_feature_width)
    far_out = jnp.einsum('qk,kd->qd', far_round, fv_full)
    context = lax.optimization_barrier((local_output + jnp.where(column_active[None, :, None], far_out[:, None, :], 0.0)).reshape(total_row_count, head_feature_width).astype(jnp.bfloat16))
    row_delta_terms = lax.optimization_barrier(jnp.sum(context.astype(jnp.float32) * full_gradient, axis=-1))
    selected_delta = lax.dynamic_index_in_dim(row_delta_terms.reshape(selected_count, FAR_DILATION), start_offset, 1, keepdims=False)
    local_probability_gradient = jnp.einsum('mhr,mtr->mht', segment_gradient, value_segment)
    local_score_gradient = rounded(near_prob * (local_probability_gradient - row_delta_terms.reshape(segments, SEGMENT)[:, :, None]) * score_scale_factor)
    far_dp = jnp.einsum('qd,kd->qk', selected_gradient, fv_full)
    far_ds = rounded(far_prob * (far_dp - selected_delta[:, None]) * score_scale_factor)
    local_query_gradient = jnp.einsum('wun,wnj->wuj', local_score_gradient, key_segment).reshape(selected_count, FAR_DILATION, head_feature_width)
    far_dq = jnp.einsum('qk,kd->qd', far_ds, fk_full)
    d_queries = (local_query_gradient + jnp.where(column_active[None, :, None], far_dq[:, None, :], 0.0)).reshape(total_row_count, head_feature_width).astype(jnp.bfloat16)
    keys_gradient = jnp.einsum('pjz,pjn->pzn', local_score_gradient, query_segment).reshape(total_row_count, head_feature_width)
    values_gradient = jnp.einsum('pjz,pjn->pzn', local_rounded, segment_gradient).reshape(total_row_count, head_feature_width)
    d_far_keys = jnp.einsum('qk,qd->kd', far_ds, query_selected)
    d_far_values = jnp.einsum('qk,qd->kd', far_round, selected_gradient)
    return (context, d_queries, keys_gradient, values_gradient, d_far_keys, d_far_values)

def reference(patches, w_query, w_key, w_value, w_out, lengths, cotangent):
    positions = jnp.arange(SPAN, dtype=jnp.int32)
    start_offsets = (jnp.arange(ATTENTION_HEADS, dtype=jnp.int32) % FAR_DILATION).astype(jnp.int32)

    def span_step(carry, slab):
        tokens, cot_rows, length = slab
        query_rows = jnp.dot(tokens, w_query, preferred_element_type=jnp.float32).astype(jnp.bfloat16)
        key_rows = jnp.dot(tokens, w_key, preferred_element_type=jnp.float32).astype(jnp.bfloat16)
        value_rows = jnp.dot(tokens, w_value, preferred_element_type=jnp.float32).astype(jnp.bfloat16)
        far_pair = pick_rows(jnp.stack([key_rows, value_rows]), ATTENTION_HEADS)
        context_gradient = jnp.dot(cot_rows, w_out.T, preferred_element_type=jnp.float32).astype(jnp.bfloat16)
        operands = (to_heads(query_rows), to_heads(key_rows), to_heads(value_rows), to_heads(far_pair[0]), to_heads(far_pair[1]), to_heads(context_gradient), start_offsets)
        context, d_queries, keys_gradient, values_gradient, d_far_keys, d_far_values = lax.map(lambda segment_member: head_pass(segment_member, positions, length), operands)
        context_all = from_heads(context)
        dq_all = from_heads(d_queries)
        dk_all = (from_heads(keys_gradient) + place_rows(from_heads(d_far_keys), ATTENTION_HEADS)).astype(jnp.bfloat16)
        dv_all = (from_heads(values_gradient) + place_rows(from_heads(d_far_values), ATTENTION_HEADS)).astype(jnp.bfloat16)
        attended = jnp.dot(context_all, w_out, preferred_element_type=jnp.float32).astype(jnp.bfloat16)
        grad_rows = (jnp.dot(dq_all, w_query.T, preferred_element_type=jnp.float32) + jnp.dot(dk_all, w_key.T, preferred_element_type=jnp.float32) + jnp.dot(dv_all, w_value.T, preferred_element_type=jnp.float32)).astype(jnp.bfloat16)
        tokens_f = tokens.astype(jnp.float32)
        terms = (jnp.einsum('rd,re->de', tokens_f, dq_all.astype(jnp.float32)), jnp.einsum('rd,re->de', tokens_f, dk_all.astype(jnp.float32)), jnp.einsum('rd,re->de', tokens_f, dv_all.astype(jnp.float32)), jnp.einsum('rd,re->de', context_all.astype(jnp.float32), cot_rows.astype(jnp.float32)))
        carry = tuple((carry[segment_member] + terms[segment_member] for segment_member in range(4)))
        return (carry, (attended, grad_rows))
    zeros = tuple((jnp.zeros((D, D), jnp.float32) for segment_member in range(4)))
    sums, outputs = lax.scan(span_step, zeros, (patches, cotangent, lengths))
    return (outputs[0], outputs[1], sums[0].astype(jnp.bfloat16), sums[1].astype(jnp.bfloat16), sums[2].astype(jnp.bfloat16), sums[3].astype(jnp.bfloat16))
```

```python
import math

import jax
import jax.numpy as jnp
from jax import lax
from jax.experimental import pallas as pl
from jax.experimental.pallas import tpu as pltpu
from jax.sharding import PartitionSpec as P

BF, F32 = jnp.bfloat16, jnp.float32
NEGATIVE = -1e30
ROWS, D, HEAD, PAIRS = 1024, 768, 64, 6
FAR = 256
LN2 = math.log(2.0)
QUERY_SCALE = 1.0 / (math.sqrt(HEAD) * LN2)
VMEM_LIMIT = 56 << 20


def nn(a, b):
    return lax.dot_general(a, b, (((1,), (0,)), ((), ())), preferred_element_type=F32)


def nt(a, b):
    return lax.dot_general(a, b, (((1,), (1,)), ((), ())), preferred_element_type=F32)


def selection(transposed):
    a = lax.broadcasted_iota(jnp.int32, (512, 512), 1 if transposed else 0)
    b = lax.broadcasted_iota(jnp.int32, (512, 512), 0 if transposed else 1)
    return jnp.where(4 * (a & 127) + (a >> 7) == b, 1.0, 0.0).astype(BF)


def project_kernel(x, cot, wq, wk, wv, wo, xp, cp, q, k, v, do, far):
    pick = selection(False)
    rows = nn(pick, x[...]).astype(BF)
    cots = nn(pick, cot[...]).astype(BF)
    qs = (nn(rows, wq[...]) * QUERY_SCALE).astype(BF)
    ks = nn(rows, wk[...]).astype(BF)
    vs = nn(rows, wv[...]).astype(BF)
    ds = nt(cots, wo[...]).astype(BF)
    for ref, value in ((xp, rows), (cp, cots), (q, qs), (k, ks), (v, vs), (do, ds)):
        for c in range(4):
            ref[c] = value[c * 128 : c * 128 + 128]
    left = lax.broadcasted_iota(jnp.int32, (128, 128), 1) < HEAD
    for n, value in ((0, ks), (1, vs)):
        for t in range(PAIRS):
            c = 2 * (t % 2)
            at = slice(t * 128, t * 128 + 128)
            far[n, :, at] = jnp.where(
                left, value[c * 128 : c * 128 + 128, at], value[c * 128 + 128 : c * 128 + 256, at]
            )


def attend_kernel(info, q, k, v, do, far, ctxT, dqT, dkT, dvT, dfar, e_scr, ds_scr, t_scr):
    pair = pl.program_id(0)
    length, base = info[0], info[1]
    zero, one = jnp.zeros((), BF), jnp.ones((), BF)
    qT, doT, kT, vT = q[...].T, do[...].T, k[...].T, v[...].T
    kf = far[:, 0].reshape(ROWS, 128)
    vf = far[:, 1].reshape(ROWS, 128)
    kfT, vfT = kf.T, vf.T
    lane = lax.broadcasted_iota(jnp.int32, (ROWS, 128), 1)
    row = lax.broadcasted_iota(jnp.int32, (ROWS, 128), 0)
    sub = lax.broadcasted_iota(jnp.int32, (128, ROWS), 0)
    near_bias = jnp.where(4 * (row & 255) + (row >> 8) + base < length, 0.0, NEGATIVE).astype(BF)
    rq = lax.broadcasted_iota(jnp.int32, (1, ROWS), 1)
    real = jnp.where(4 * (rq & 255) + (rq >> 8) + base < length, 1.0, 0.0)
    tail = jnp.where(lax.broadcasted_iota(jnp.int32, (16, ROWS), 0) == 0, 1.0, 0.0).astype(BF)
    for a in range(2):
        o = HEAD * (1 - a)
        c = 2 * (pair & 1) + a
        mine = (lane < HEAD) if a == 0 else (lane >= HEAD)
        mine_t = (sub < HEAD) if a == 0 else (sub >= HEAD)
        sl = slice(HEAD * a, HEAD * a + HEAD)
        far_bias = jnp.where(4 * row + c < length, 0.0, NEGATIVE).astype(BF)
        ones2 = jnp.where((lane == o) | (lane == o + 1), one, zero)
        ka = jnp.where(mine, k[...], jnp.where(lane == o, near_bias, zero))
        kfa = jnp.where(mine, kf, jnp.where(lane == o, far_bias, zero))
        va = jnp.where(mine, v[...], ones2)
        vfa = jnp.where(mine, vf, ones2)
        t_scr[1] = jnp.where(mine_t, qT, jnp.where(sub == o, one, zero))
        t_scr[2] = doT
        t_scr[3, 0:1, :] = real.astype(BF)
        vta = jnp.concatenate([vT[sl], tail], axis=0)
        vfta = jnp.concatenate([vfT[sl], tail], axis=0)
        kta, kfta = kT[sl], kfT[sl]
        for b in range(4):
            at = pl.ds(pl.multiple_of(((c + b) & 3) * 256, 256), 256)
            qb = t_scr[1, :, at]
            s = nn(ka, qb)
            peak = jnp.max(s, axis=0, keepdims=True)
            if b == 0:
                sf = nn(kfa, qb)
                peak = jnp.maximum(peak, jnp.max(sf, axis=0, keepdims=True))
            e = jnp.exp2(s - peak).astype(BF)
            out = nn(vta, e)
            if b == 0:
                ef = jnp.exp2(sf - peak).astype(BF)
                out = out + nn(vfta, ef)
            weight = t_scr[3, 0:1, at].astype(F32) / out[HEAD : HEAD + 1]
            cx = (out[:HEAD] * weight).astype(BF)
            ctxT[sl, at] = cx
            dob = t_scr[2, sl, at].astype(F32)
            shift = -weight * jnp.sum(cx.astype(F32) * dob, axis=0, keepdims=True)
            high = shift.astype(BF)
            low = (shift - high.astype(F32)).astype(BF)
            dw = (dob * weight).astype(BF)
            sub2 = lax.broadcasted_iota(jnp.int32, (HEAD, 256), 0)
            extra = jnp.where(sub2 == 0, high, jnp.where(sub2 == 1, low, zero))
            dwa = jnp.concatenate([dw, extra] if a == 0 else [extra, dw], axis=0)
            ds = e * nn(va, dwa).astype(BF)
            dq = nn(kta, ds)
            if b == 0:
                dsf = ef * nn(vfa, dwa).astype(BF)
                dq = dq + nn(kfta, dsf)
                dfk = (nt(qb[sl], dsf) * LN2).astype(BF)
                dfv = nt(dw, ef).astype(BF)
                for j in range(4):
                    dfar[j, 0, sl, :] = dfk[:, j * FAR : j * FAR + FAR]
                    dfar[j, 1, sl, :] = dfv[:, j * FAR : j * FAR + FAR]
            dqT[sl, at] = (dq * 0.125).astype(BF)
            e_scr[:, at] = e
            ds_scr[:, at] = ds
            t_scr[0, sl, at] = dw
        dkT[sl, :] = nt(t_scr[1, sl, :], ds_scr[...]) * LN2
        dvT[sl, :] = nt(t_scr[0, sl, :], e_scr[...])


def finish_kernel(ctxT, dqT, dkT, dvT, own, xp, cp, wq, wk, wv, wo, att, gx, grads, dkb, dvb):
    for h in range(2 * PAIRS):
        sl = slice(h * HEAD, h * HEAD + HEAD)
        c = h % 4
        for n, (src, dst) in enumerate(((dkT, dkb), (dvT, dvb))):
            for b in range(4):
                at = slice(b * FAR, b * FAR + FAR)
                value = src[sl, at]
                if b == c:
                    value = value + own[n, sl, :].astype(F32)
                dst[sl, at] = value.astype(BF)
    grads[3] = nn(ctxT[...], cp[...])
    grads[0] = nn(dqT[...], xp[...])
    grads[1] = nn(dkb[...], xp[...])
    grads[2] = nn(dvb[...], xp[...])
    place = selection(True)
    woT = wo[...].T
    for j in range(2):
        def part(ref):
            return jnp.concatenate(
                [ref[:, c * FAR + j * 128 : c * FAR + j * 128 + 128] for c in range(4)], axis=1
            )

        outT = nn(woT, part(ctxT)).astype(BF)
        att[j * 512 : j * 512 + 512, :] = nt(place, outT).astype(BF)
        gT = nn(wq[...], part(dqT)) + nn(wk[...], part(dkb)) + nn(wv[...], part(dvb))
        gx[j * 512 : j * 512 + 512, :] = nt(place, gT.astype(BF)).astype(BF)


def project(tokens, cots, wq, wk, wv, wo):
    rows = pl.BlockSpec((512, D), lambda j: (j, 0))
    whole = pl.BlockSpec((D, D), lambda j: (0, 0))
    out = pl.BlockSpec((4, 128, D), lambda j: (0, j, 0))
    shape = jax.ShapeDtypeStruct((4, FAR, D), BF)
    return pl.pallas_call(
        project_kernel,
        grid=(2,),
        in_specs=[rows, rows, whole, whole, whole, whole],
        out_specs=[out] * 6 + [pl.BlockSpec((2, 128, D), lambda j: (0, j, 0))],
        out_shape=[shape] * 6 + [jax.ShapeDtypeStruct((2, FAR, D), BF)],
        compiler_params=pltpu.CompilerParams(vmem_limit_bytes=VMEM_LIMIT),
    )(tokens, cots, wq, wk, wv, wo)


def attend(info, q, k, v, do, far):
    col = pl.BlockSpec((ROWS, 128), lambda i: (0, i))
    row = pl.BlockSpec((128, ROWS), lambda i: (i, 0))
    return pl.pallas_call(
        attend_kernel,
        grid=(PAIRS,),
        in_specs=[
            pl.BlockSpec(memory_space=pltpu.SMEM),
            col,
            col,
            col,
            col,
            pl.BlockSpec((4, 2, FAR, 128), lambda i: (0, 0, 0, i)),
        ],
        out_specs=[row, row, row, row, pl.BlockSpec((4, 2, 128, FAR), lambda i: (0, 0, i, 0))],
        out_shape=[
            jax.ShapeDtypeStruct((D, ROWS), BF),
            jax.ShapeDtypeStruct((D, ROWS), BF),
            jax.ShapeDtypeStruct((D, ROWS), F32),
            jax.ShapeDtypeStruct((D, ROWS), F32),
            jax.ShapeDtypeStruct((4, 2, D, FAR), BF),
        ],
        scratch_shapes=[
            pltpu.VMEM((ROWS, ROWS), BF),
            pltpu.VMEM((ROWS, ROWS), BF),
            pltpu.VMEM((4, 128, ROWS), BF),
        ],
        compiler_params=pltpu.CompilerParams(vmem_limit_bytes=VMEM_LIMIT),
    )(info, q, k, v, do, far)


def finish(*operands):
    return pl.pallas_call(
        finish_kernel,
        out_shape=[
            jax.ShapeDtypeStruct((ROWS, D), BF),
            jax.ShapeDtypeStruct((ROWS, D), BF),
            jax.ShapeDtypeStruct((4, D, D), F32),
        ],
        scratch_shapes=[pltpu.VMEM((D, ROWS), BF), pltpu.VMEM((D, ROWS), BF)],
        compiler_params=pltpu.CompilerParams(vmem_limit_bytes=VMEM_LIMIT),
    )(*operands)


def local(patches, wq, wk, wv, wo, lengths, cotangent):
    base = lax.axis_index("seq").astype(jnp.int32) * ROWS
    info = jnp.stack([lengths[0], base])
    xp, cp, q, k, v, do, far = project(patches[0], cotangent[0], wq, wk, wv, wo)
    flat = lambda t: t.reshape(ROWS, D)
    far_all = lax.all_gather(far, "seq", axis=0)
    ctxT, dqT, dkT, dvT, dfar = attend(info, flat(q), flat(k), flat(v), flat(do), far_all)
    own = lax.psum_scatter(dfar, "seq", scatter_dimension=0, tiled=False)
    att, gx, grads = finish(ctxT, dqT, dkT, dvT, own, flat(xp), flat(cp), wq, wk, wv, wo)
    totals = lax.psum(grads, ("seq", "slide")).astype(BF)
    return (att[None], gx[None], totals[0].T, totals[1].T, totals[2].T, totals[3])


def solution(mesh):
    split = P("slide", "seq", None)
    return jax.shard_map(
        local,
        mesh=mesh,
        in_specs=(split, P(), P(), P(), P(), P("slide"), split),
        out_specs=(split, split, P(), P(), P(), P()),
        check_vma=False,
    )
```

```python
import math

import jax
import jax.numpy as jnp
from jax import lax
from jax.experimental import pallas as pl
from jax.experimental.pallas import tpu as pltpu
from jax.sharding import PartitionSpec as P

BF, F32 = jnp.bfloat16, jnp.float32
MESH = pl.DeviceIdType.MESH
NEGATIVE = -1e30
ROWS, D, HEAD, PAIRS = 1024, 768, 64, 6
FAR = 256
LN2 = math.log(2.0)
QUERY_SCALE = 1.0 / (math.sqrt(HEAD) * LN2)
VMEM_LIMIT = 60 << 20
PART, HALF, QUARTER, PIECE = 3072, 1536, 384, 96


def nn(a, b):
    return lax.dot_general(a, b, (((1,), (0,)), ((), ())), preferred_element_type=F32)


def nt(a, b):
    return lax.dot_general(a, b, (((1,), (1,)), ((), ())), preferred_element_type=F32)


def selection(transposed):
    a = lax.broadcasted_iota(jnp.int32, (512, 512), 1 if transposed else 0)
    b = lax.broadcasted_iota(jnp.int32, (512, 512), 0 if transposed else 1)
    return jnp.where(4 * (a & 127) + (a >> 7) == b, 1.0, 0.0).astype(BF)


def kernel(
    info, x_hbm, cot_hbm, wq_hbm, wk_hbm, wv_hbm, wo_hbm,
    att_hbm, gx_hbm, total,
    wq, wk, wv, wo, xpT, cp, q, k, v, do, far,
    ctxT, dqT, dkT, dvT, e_scr, ds_scr, t_scr, near,
    dfs, dfr, part, ar, bs, br, cs, xr, zr, fin,
    load_sem, far_s, far_r, df_s, df_r, a_s, a_r, b_s, b_r, x_s, x_r, z_s, z_r,
    gx_s, gx_r, gl_s, gy_s, gy_r, gc_s, gc_r, out_sem,
):
    y = lax.axis_index("seq").astype(jnp.int32)
    slide = lax.axis_index("slide").astype(jnp.int32)
    xi = lax.div(slide, 8)
    zi = lax.rem(lax.div(slide, 2), 4)
    core = lax.rem(slide, 2)
    length = info[0]
    base = y * ROWS

    def y_peer(n):
        return (lax.rem(y + n, 4), slide)

    def x_peer(n):
        return (y, slide + 8 * (lax.rem(xi + n, 4) - xi))

    def z_peer(n):
        return (y, slide + 2 * (lax.rem(zi + n, 4) - zi))

    sibling = (y, slide + 1 - 2 * core)

    loads = [
        pltpu.make_async_copy(src, dst, load_sem.at[n])
        for n, (src, dst) in enumerate(
            (
                (x_hbm, e_scr.at[:, 0:D]),
                (wk_hbm, wk),
                (wv_hbm, wv),
                (cot_hbm, ds_scr.at[:, 0:D]),
                (wo_hbm, wo),
                (wq_hbm, wq),
            )
        )
    ]
    for copy in loads:
        copy.start()
    barrier = pltpu.get_barrier_semaphore()
    peers = [sibling] + [f(n) for f in (y_peer, x_peer, z_peer) for n in (1, 2, 3)]
    for peer in peers:
        pl.semaphore_signal(barrier, inc=1, device_id=peer, device_id_type=MESH)

    def remote(src, dst, send, recv, peer):
        return pltpu.make_async_remote_copy(
            src_ref=src, dst_ref=dst, send_sem=send, recv_sem=recv, device_id=peer, device_id_type=MESH
        )

    def ds(start, size, step):
        return pl.ds(pl.multiple_of(start, step), size)

    def far_copy(p, n, src):
        return remote(far.at[src, p], far.at[src, p], far_s.at[n - 1, p], far_r.at[n - 1, p], y_peer(n))

    def df_copy(p, n):
        block = dfs.at[lax.rem(p, 2), lax.rem(y + n, 4)]
        return remote(block, dfr.at[p, n - 1], df_s.at[n - 1, p], df_r.at[n - 1, p], y_peer(n))

    def a_copy(p):
        block = part.at[lax.rem(p, 2), ds((1 - core) * HALF, HALF, HALF)]
        return remote(block, ar.at[p], a_s.at[p], a_r.at[p], sibling)

    def b_copy(p, n):
        block = bs.at[lax.rem(p, 2), ds(lax.rem(y + n, 4) * QUARTER, QUARTER, QUARTER)]
        return remote(block, br.at[p, n - 1], b_s.at[n - 1, p], b_r.at[n - 1, p], y_peer(n))

    def x_copy(p, n):
        block = cs.at[lax.rem(p, 2), ds(lax.rem(xi + n, 4) * PIECE, PIECE, PIECE)]
        return remote(block, xr.at[p, n - 1], x_s.at[n - 1, p], x_r.at[n - 1, p], x_peer(n))

    def z_copy(p, n, src):
        return remote(zr.at[p, src], zr.at[p, src], z_s.at[n - 1, p], z_r.at[n - 1, p], z_peer(n))

    def gx_copy(p, n, src):
        block = total.at[p, ds(core * HALF + y * QUARTER + src * PIECE, PIECE, PIECE)]
        return remote(fin.at[p], block, gx_s.at[n - 1, p], gx_r.at[n - 1, p], x_peer(n))

    def gl_copy(p):
        block = total.at[p, ds(core * HALF + y * QUARTER + xi * PIECE, PIECE, PIECE)]
        return pltpu.make_async_copy(fin.at[p], block, gl_s.at[p])

    def gy_copy(p, n, src):
        block = total.at[p, ds(core * HALF + src * QUARTER, QUARTER, QUARTER)]
        return remote(block, block, gy_s.at[n - 1, p], gy_r.at[n - 1, p], y_peer(n))

    def gc_copy(p, src):
        block = total.at[p, ds(src * HALF, HALF, HALF)]
        return remote(block, block, gc_s.at[p], gc_r.at[p], sibling)

    def back(index, n):
        return lax.rem(index + 4 - n, 4)

    pick = selection(False)
    left = lax.broadcasted_iota(jnp.int32, (128, 128), 1) < HEAD

    def spread(ref, j, value):
        for c in range(4):
            ref[c * FAR + j * 128 : c * FAR + j * 128 + 128, :] = value[c * 128 : c * 128 + 128]

    loads[0].wait()
    loads[1].wait()
    loads[2].wait()
    rows = []
    for j in range(2):
        block = nn(pick, e_scr[j * 512 : j * 512 + 512, 0:D]).astype(BF)
        rows.append(block)
        for n, (w, ref) in enumerate(((wk, k), (wv, v))):
            value = nn(block, w[...]).astype(BF)
            spread(ref, j, value)
            for t in range(PAIRS):
                c = 256 * (t % 2)
                at = slice(t * 128, t * 128 + 128)
                far[y, t, n, j * 128 : j * 128 + 128, :] = jnp.where(
                    left, value[c : c + 128, at], value[c + 128 : c + 256, at]
                )
    pl.semaphore_wait(barrier, len(peers))
    for p in range(PAIRS):
        for n in (1, 2, 3):
            far_copy(p, n, y).start()
    loads[3].wait()
    loads[4].wait()
    loads[5].wait()
    for j in range(2):
        spread(q, j, (nn(rows[j], wq[...]) * QUERY_SCALE).astype(BF))
        blockT = rows[j].T
        for c in range(4):
            xpT[:, c * FAR + j * 128 : c * FAR + j * 128 + 128] = blockT[:, c * 128 : c * 128 + 128]
        block = nn(pick, ds_scr[j * 512 : j * 512 + 512, 0:D]).astype(BF)
        spread(cp, j, block)
        spread(do, j, nt(block, wo[...]).astype(BF))

    zero, one = jnp.zeros((), BF), jnp.ones((), BF)

    def prepare(i):
        at = ds(i * 128, 128, 128)
        for n in (1, 2, 3):
            far_copy(i, n, back(y, n)).wait_recv()
        t_scr[2] = do[:, at].T
        t_scr[4] = q[:, at].T
        t_scr[5] = k[:, at].T
        t_scr[6] = v[:, at].T
        for s in range(4):
            t_scr[7, :, s * FAR : s * FAR + FAR] = far[s, i, 0].T
            t_scr[8, :, s * FAR : s * FAR + FAR] = far[s, i, 1].T

    def attend(i, a):
        slot = lax.rem(i, 2)
        lanes = ds(i * 128, 128, 128)
        lane = lax.broadcasted_iota(jnp.int32, (ROWS, 128), 1)
        row = lax.broadcasted_iota(jnp.int32, (ROWS, 128), 0)
        sub = lax.broadcasted_iota(jnp.int32, (128, ROWS), 0)
        near_bias = jnp.where(4 * (row & 255) + (row >> 8) + base < length, 0.0, NEGATIVE).astype(BF)
        rq = lax.broadcasted_iota(jnp.int32, (1, ROWS), 1)
        real = jnp.where(4 * (rq & 255) + (rq >> 8) + base < length, 1.0, 0.0)
        tail = jnp.where(lax.broadcasted_iota(jnp.int32, (16, ROWS), 0) == 0, 1.0, 0.0).astype(BF)
        o = HEAD * (1 - a)
        c = 2 * lax.rem(i, 2) + a
        mine = (lane < HEAD) if a == 0 else (lane >= HEAD)
        mine_t = (sub < HEAD) if a == 0 else (sub >= HEAD)
        sl = slice(HEAD * a, HEAD * a + HEAD)
        far_bias = jnp.where(4 * row + c < length, 0.0, NEGATIVE).astype(BF)
        ones2 = jnp.where((lane == o) | (lane == o + 1), one, zero)
        kf = far[:, i, 0].reshape(ROWS, 128)
        vf = far[:, i, 1].reshape(ROWS, 128)
        ka = jnp.where(mine, k[:, lanes], jnp.where(lane == o, near_bias, zero))
        kfa = jnp.where(mine, kf, jnp.where(lane == o, far_bias, zero))
        va = jnp.where(mine, v[:, lanes], ones2)
        vfa = jnp.where(mine, vf, ones2)
        t_scr[1] = jnp.where(mine_t, t_scr[4], jnp.where(sub == o, one, zero))
        t_scr[3, 0:1, :] = real.astype(BF)
        vta = jnp.concatenate([t_scr[6, sl, :], tail], axis=0)
        vfta = jnp.concatenate([t_scr[8, sl, :], tail], axis=0)
        kta, kfta = t_scr[5, sl, :], t_scr[7, sl, :]
        for b in range(4):
            at = ds(lax.rem(c + b, 4) * 256, 256, 256)
            qb = t_scr[1, :, at]
            s = nn(ka, qb)
            peak = jnp.max(s, axis=0, keepdims=True)
            if b == 0:
                sf = nn(kfa, qb)
                peak = jnp.maximum(peak, jnp.max(sf, axis=0, keepdims=True))
            e = jnp.exp2(s - peak).astype(BF)
            out = nn(vta, e)
            if b == 0:
                ef = jnp.exp2(sf - peak).astype(BF)
                out = out + nn(vfta, ef)
            weight = t_scr[3, 0:1, at].astype(F32) / out[HEAD : HEAD + 1]
            cx = (out[:HEAD] * weight).astype(BF)
            ctxT[i, sl, at] = cx
            dob = t_scr[2, sl, at].astype(F32)
            shift = -weight * jnp.sum(cx.astype(F32) * dob, axis=0, keepdims=True)
            high = shift.astype(BF)
            low = (shift - high.astype(F32)).astype(BF)
            dw = (dob * weight).astype(BF)
            sub2 = lax.broadcasted_iota(jnp.int32, (HEAD, 256), 0)
            extra = jnp.where(sub2 == 0, high, jnp.where(sub2 == 1, low, zero))
            dwa = jnp.concatenate([dw, extra] if a == 0 else [extra, dw], axis=0)
            dsc = e * nn(va, dwa).astype(BF)
            dq = nn(kta, dsc)
            if b == 0:
                dsf = ef * nn(vfa, dwa).astype(BF)
                dq = dq + nn(kfta, dsf)
                dfk = (nt(qb[sl], dsf) * LN2).astype(BF)
                dfv = nt(dw, ef).astype(BF)
                for j in range(4):
                    dfs[slot, j, 0, sl, :] = dfk[:, j * FAR : j * FAR + FAR]
                    dfs[slot, j, 1, sl, :] = dfv[:, j * FAR : j * FAR + FAR]
            dqT[i, sl, at] = (dq * 0.125).astype(BF)
            e_scr[:, at] = e
            ds_scr[:, at] = dsc
            t_scr[0, sl, at] = dw
        near[slot, 0, sl, :] = nt(t_scr[1, sl, :], ds_scr[...]) * LN2
        near[slot, 1, sl, :] = nt(t_scr[0, sl, :], e_scr[...])

    def send_far_grads(p):
        for n in (1, 2, 3):
            df_copy(p, n).start()

    def weigh(p):
        slot = lax.rem(p, 2)
        for n in (1, 2, 3):
            df_copy(p, n).wait()
        for a in range(2):
            sl = slice(HEAD * a, HEAD * a + HEAD)
            at = ds((2 * slot + a) * FAR, FAR, FAR)
            for n, dst in ((0, dkT), (1, dvT)):
                own = dfs[slot, y, n, sl, :].astype(F32)
                for m in range(3):
                    own = own + dfr[p, m, n, sl, :].astype(F32)
                dst[p, sl, :] = near[slot, n, sl, :].astype(BF)
                dst[p, sl, at] = (near[slot, n, sl, at] + own).astype(BF)
        for n, src in enumerate((dqT, dkT, dvT)):
            part[slot, n * D : n * D + D, :] = nt(xpT[...], src[p]).astype(BF)
        gout = nn(ctxT[p], cp[...]).astype(BF)
        for t in range(6):
            at = 3 * D + t * 128
            part[slot, at : at + 128, :] = gout[:, t * 128 : t * 128 + 128]
        a_copy(p).start()

    def sum_core(p):
        slot = lax.rem(p, 2)
        a_copy(p).wait()
        mine = part[slot, ds(core * HALF, HALF, HALF), :]
        bs[slot] = (mine.astype(F32) + ar[p].astype(F32)).astype(BF)
        for n in (1, 2, 3):
            b_copy(p, n).start()

    def sum_y(p):
        slot = lax.rem(p, 2)
        for n in (1, 2, 3):
            b_copy(p, n).wait()
        acc = bs[slot, ds(y * QUARTER, QUARTER, QUARTER), :].astype(F32)
        for n in range(3):
            acc = acc + br[p, n].astype(F32)
        cs[slot] = acc.astype(BF)
        for n in (1, 2, 3):
            x_copy(p, n).start()

    def sum_x(p):
        slot = lax.rem(p, 2)
        for n in (1, 2, 3):
            x_copy(p, n).wait()
        acc = cs[slot, ds(xi * PIECE, PIECE, PIECE), :].astype(F32)
        for n in range(3):
            acc = acc + xr[p, n].astype(F32)
        zr[p, zi] = acc.astype(BF)
        for n in (1, 2, 3):
            z_copy(p, n, zi).start()

    def sum_z(p):
        for n in (1, 2, 3):
            z_copy(p, n, zi).wait_send()
            z_copy(p, n, back(zi, n)).wait_recv()
        acc = zr[p, 0].astype(F32)
        for n in (1, 2, 3):
            acc = acc + zr[p, n].astype(F32)
        fin[p] = acc.astype(BF)
        gl_copy(p).start()
        for n in (1, 2, 3):
            gx_copy(p, n, xi).start()

    def gather_y(p):
        gl_copy(p).wait()
        for n in (1, 2, 3):
            gx_copy(p, n, xi).wait_send()
            gx_copy(p, n, back(xi, n)).wait_recv()
        for n in (1, 2, 3):
            gy_copy(p, n, y).start()

    def gather_core(p):
        for n in (1, 2, 3):
            gy_copy(p, n, y).wait_send()
            gy_copy(p, n, back(y, n)).wait_recv()
        gc_copy(p, core).start()

    def end(p):
        gc_copy(p, core).wait_send()
        gc_copy(p, 1 - core).wait_recv()

    first = ((weigh, 1), (sum_y, 2), (sum_z, 3), (gather_core, 4))
    second = ((sum_core, 1), (sum_x, 2), (gather_y, 3), (end, 4))

    def step(i, carry):
        prepare(i)
        attend(i, 0)
        for run, lag in first:
            pl.when(i >= lag)(lambda run=run, lag=lag: run(i - lag))
        attend(i, 1)
        send_far_grads(i)
        for run, lag in second:
            pl.when(i >= lag)(lambda run=run, lag=lag: run(i - lag))
        return carry

    lax.fori_loop(0, PAIRS, step, 0)

    place = selection(True)

    def cols(ref, j):
        return jnp.concatenate(
            [ref[:, :, c * FAR + j * 128 : c * FAR + j * 128 + 128].reshape(D, 128) for c in range(4)], axis=1
        )

    def attended(j):
        outT = nn(wo[...].T, cols(ctxT, j)).astype(BF)
        q[j * 512 : j * 512 + 512, :] = nt(place, outT).astype(BF)

    def patch_grads(j):
        gT = nn(wq[...], cols(dqT, j)) + nn(wk[...], cols(dkT, j)) + nn(wv[...], cols(dvT, j))
        k[j * 512 : j * 512 + 512, :] = nt(place, gT.astype(BF)).astype(BF)

    att_copy = pltpu.make_async_copy(q, att_hbm, out_sem.at[0])
    grad_copy = pltpu.make_async_copy(k, gx_hbm, out_sem.at[1])

    sum_y(4)
    sum_z(3)
    gather_core(2)
    attended(0)
    weigh(5)
    sum_x(4)
    gather_y(3)
    end(2)
    attended(1)
    att_copy.start()
    sum_core(5)
    sum_z(4)
    gather_core(3)
    patch_grads(0)
    sum_y(5)
    gather_y(4)
    end(3)
    patch_grads(1)
    grad_copy.start()
    sum_x(5)
    gather_core(4)
    sum_z(5)
    end(4)
    gather_y(5)
    gather_core(5)
    end(5)
    att_copy.wait()
    grad_copy.wait()
    for p in range(PAIRS):
        for n in (1, 2, 3):
            far_copy(p, n, y).wait_send()


def sublayer(info, x, cot, wq, wk, wv, wo):
    anywhere = pl.BlockSpec(memory_space=pl.ANY)
    dma = pltpu.SemaphoreType.DMA
    three, each = dma((3, PAIRS)), dma((PAIRS,))
    scratch = [
        *[pltpu.VMEM((D, D), BF)] * 4,
        pltpu.VMEM((D, ROWS), BF),
        pltpu.VMEM((ROWS, D), BF),
        *[pltpu.VMEM((ROWS, D), BF)] * 4,
        pltpu.VMEM((4, PAIRS, 2, FAR, 128), BF),
        *[pltpu.VMEM((PAIRS, 128, ROWS), BF)] * 4,
        pltpu.VMEM((ROWS, ROWS), BF),
        pltpu.VMEM((ROWS, ROWS), BF),
        pltpu.VMEM((9, 128, ROWS), BF),
        pltpu.VMEM((2, 2, 128, ROWS), F32),
        pltpu.VMEM((2, 4, 2, 128, FAR), BF),
        pltpu.VMEM((PAIRS, 3, 2, 128, FAR), BF),
        pltpu.VMEM((2, PART, 128), BF),
        pltpu.VMEM((PAIRS, HALF, 128), BF),
        pltpu.VMEM((2, HALF, 128), BF),
        pltpu.VMEM((PAIRS, 3, QUARTER, 128), BF),
        pltpu.VMEM((2, QUARTER, 128), BF),
        pltpu.VMEM((PAIRS, 3, PIECE, 128), BF),
        pltpu.VMEM((PAIRS, 4, PIECE, 128), BF),
        pltpu.VMEM((PAIRS, PIECE, 128), BF),
        dma((6,)),
        three, three, three, three, each, each, three, three, three, three, three, three,
        three, three, each, three, three, each, each, dma((2,)),
    ]
    return pl.pallas_call(
        kernel,
        in_specs=[pl.BlockSpec(memory_space=pltpu.SMEM)] + [anywhere] * 6,
        out_specs=[anywhere] * 3,
        out_shape=[
            jax.ShapeDtypeStruct((ROWS, D), BF),
            jax.ShapeDtypeStruct((ROWS, D), BF),
            jax.ShapeDtypeStruct((PAIRS, PART, 128), BF),
        ],
        scratch_shapes=scratch,
        compiler_params=pltpu.CompilerParams(
            vmem_limit_bytes=VMEM_LIMIT, collective_id=0, has_side_effects=True
        ),
    )(info, x, cot, wq, wk, wv, wo)


def local(patches, wq, wk, wv, wo, lengths, cotangent):
    att, gx, total = sublayer(lengths, patches[0], cotangent[0], wq, wk, wv, wo)
    columns = [
        total[:, n * D : n * D + D].transpose(1, 0, 2).reshape(D, D) for n in range(3)
    ]
    rows = total[:, 3 * D :].reshape(PAIRS, PAIRS, 128, 128).transpose(0, 2, 1, 3).reshape(D, D)
    return (att[None], gx[None], *columns, rows)


def solution(mesh):
    split = P("slide", "seq", None)
    return jax.shard_map(
        local,
        mesh=mesh,
        in_specs=(split, P(), P(), P(), P(), P("slide"), split),
        out_specs=(split, split, P(), P(), P(), P()),
        check_vma=False,
    )
```

```python
import math

import jax
import jax.numpy as jnp
from jax import lax
from jax.experimental import pallas as pl
from jax.experimental.pallas import tpu as pltpu
from jax.sharding import PartitionSpec as P

BF, F32 = jnp.bfloat16, jnp.float32
MESH = pl.DeviceIdType.MESH
NEGATIVE = -1e30
ROWS, D, HEAD, PAIRS = 1024, 768, 64, 6
FAR = 256
LN2 = math.log(2.0)
QUERY_SCALE = 1.0 / (math.sqrt(HEAD) * LN2)
VMEM_LIMIT = 60 << 20
PART, HALF, PIECE = 3072, 1536, 96
PLANE = 16


def nn(a, b):
    return lax.dot_general(a, b, (((1,), (0,)), ((), ())), preferred_element_type=F32)


def nt(a, b):
    return lax.dot_general(a, b, (((1,), (1,)), ((), ())), preferred_element_type=F32)


def selection(transposed):
    a = lax.broadcasted_iota(jnp.int32, (512, 512), 1 if transposed else 0)
    b = lax.broadcasted_iota(jnp.int32, (512, 512), 0 if transposed else 1)
    return jnp.where(4 * (a & 127) + (a >> 7) == b, 1.0, 0.0).astype(BF)


def kernel(
    info, x_hbm, cot_hbm, wq_hbm, wk_hbm, wv_hbm, wo_hbm,
    att_hbm, gx_hbm, total,
    wq, wk, wv, wo, xpT, cp, q, k, v, do, far,
    ctxT, dqT, dkT, dvT, e_scr, ds_scr, t_scr, o_scr, near,
    dfs, dfr, part, ar, bs, br, yr, fin,
    load_sem, far_s, far_r, df_s, df_r, a_s, a_r, b_s, b_r, y_s, y_r,
    g_s, g_r, gl_s, gc_s, gc_r, out_sem,
):
    y = lax.axis_index("seq").astype(jnp.int32)
    slide = lax.axis_index("slide").astype(jnp.int32)
    spot = lax.div(slide, 2)
    core = lax.rem(slide, 2)
    length = info[0]
    base = y * ROWS

    def y_peer(n):
        return (lax.rem(y + n, 4), slide)

    def plane_peer(n):
        return (y, 2 * lax.rem(spot + n, PLANE) + core)

    sibling = (y, slide + 1 - 2 * core)

    loads = [
        pltpu.make_async_copy(src, dst, load_sem.at[n])
        for n, (src, dst) in enumerate(
            (
                (x_hbm, e_scr.at[:, 0:D]),
                (wk_hbm, wk),
                (wv_hbm, wv),
                (cot_hbm, ds_scr.at[:, 0:D]),
                (wo_hbm, wo),
                (wq_hbm, wq),
            )
        )
    ]
    for copy in loads:
        copy.start()
    barrier = pltpu.get_barrier_semaphore()
    peers = [sibling] + [y_peer(n) for n in (1, 2, 3)] + [plane_peer(n) for n in range(1, PLANE)]
    for peer in peers:
        pl.semaphore_signal(barrier, inc=1, device_id=peer, device_id_type=MESH)

    def remote(src, dst, send, recv, peer):
        return pltpu.make_async_remote_copy(
            src_ref=src, dst_ref=dst, send_sem=send, recv_sem=recv, device_id=peer, device_id_type=MESH
        )

    def ds(start, size, step):
        return pl.ds(pl.multiple_of(start, step), size)

    def far_copy(p, n, src):
        return remote(far.at[src, p], far.at[src, p], far_s.at[n - 1, p], far_r.at[n - 1, p], y_peer(n))

    def df_copy(p, a, n):
        block = dfs.at[lax.rem(p, 2), a, lax.rem(y + n, 4)]
        return remote(block, dfr.at[p, a, n - 1], df_s.at[a, n - 1, p], df_r.at[a, n - 1, p], y_peer(n))

    def a_copy(p):
        block = part.at[lax.rem(p, 2), ds((1 - core) * HALF, HALF, HALF)]
        return remote(block, ar.at[p], a_s.at[p], a_r.at[p], sibling)

    def b_copy(p, n):
        block = bs.at[lax.rem(p, 2), ds(lax.rem(spot + n, PLANE) * PIECE, PIECE, PIECE)]
        return remote(block, br.at[p, n - 1], b_s.at[p], b_r.at[p], plane_peer(n))

    def b_all(p):
        block = br.at[p]
        return remote(block, block, b_s.at[p], b_r.at[p], sibling)

    def y_copy(p, n, src):
        return remote(yr.at[p, src], yr.at[p, src], y_s.at[n - 1, p], y_r.at[n - 1, p], y_peer(n))

    def g_copy(p, n):
        block = total.at[p, ds(core * HALF + spot * PIECE, PIECE, PIECE)]
        return remote(fin.at[p], block, g_s.at[p], g_r.at[p], plane_peer(n))

    def g_all(p):
        block = total.at[p, 0 : HALF - PIECE]
        return remote(block, block, g_s.at[p], g_r.at[p], sibling)

    def gl_copy(p):
        block = total.at[p, ds(core * HALF + spot * PIECE, PIECE, PIECE)]
        return pltpu.make_async_copy(fin.at[p], block, gl_s.at[p])

    def gc_copy(p, src):
        block = total.at[p, ds(src * HALF, HALF, HALF)]
        return remote(block, block, gc_s.at[p], gc_r.at[p], sibling)

    def to_plane(copy, p):
        def one(n, carry):
            copy(p, n).start()
            return carry

        lax.fori_loop(1, PLANE, one, 0)

    def back(index, n):
        return lax.rem(index + 4 - n, 4)

    def send_far(p):
        for n in (1, 2, 3):
            far_copy(p, n, y).start()

    pick = selection(False)
    left = lax.broadcasted_iota(jnp.int32, (128, 128), 1) < HEAD

    def spread(ref, j, value):
        for c in range(4):
            ref[c * FAR + j * 128 : c * FAR + j * 128 + 128, :] = value[c * 128 : c * 128 + 128]

    loads[0].wait()
    loads[1].wait()
    loads[2].wait()
    rows = []
    for j in range(2):
        block = nn(pick, e_scr[j * 512 : j * 512 + 512, 0:D]).astype(BF)
        rows.append(block)
        for n, (w, ref) in enumerate(((wk, k), (wv, v))):
            value = nn(block, w[...]).astype(BF)
            spread(ref, j, value)
            for t in range(PAIRS):
                c = 256 * (t % 2)
                at = slice(t * 128, t * 128 + 128)
                far[y, t, n, j * 128 : j * 128 + 128, :] = jnp.where(
                    left, value[c : c + 128, at], value[c + 128 : c + 256, at]
                )
    pl.semaphore_wait(barrier, len(peers))
    send_far(0)
    loads[3].wait()
    loads[4].wait()
    loads[5].wait()
    for j in range(2):
        spread(q, j, (nn(rows[j], wq[...]) * QUERY_SCALE).astype(BF))
        blockT = rows[j].T
        for c in range(4):
            xpT[:, c * FAR + j * 128 : c * FAR + j * 128 + 128] = blockT[:, c * 128 : c * 128 + 128]
        block = nn(pick, ds_scr[j * 512 : j * 512 + 512, 0:D]).astype(BF)
        spread(cp, j, block)
        spread(do, j, nt(block, wo[...]).astype(BF))

    send_far(1)
    zero, one = jnp.zeros((), BF), jnp.ones((), BF)

    def prepare(i):
        at = ds(i * 128, 128, 128)
        t_scr[2] = do[:, at].T
        t_scr[4] = q[:, at].T
        t_scr[5] = k[:, at].T
        t_scr[6] = v[:, at].T

    def receive(i):
        for n in (1, 2, 3):
            far_copy(i, n, back(y, n)).wait_recv()
        for s in range(4):
            t_scr[7, :, s * FAR : s * FAR + FAR] = far[s, i, 0].T
            t_scr[8, :, s * FAR : s * FAR + FAR] = far[s, i, 1].T

    def attend(i, a):
        slot = lax.rem(i, 2)
        lanes = ds(i * 128, 128, 128)
        lane = lax.broadcasted_iota(jnp.int32, (ROWS, 128), 1)
        row = lax.broadcasted_iota(jnp.int32, (ROWS, 128), 0)
        sub = lax.broadcasted_iota(jnp.int32, (128, ROWS), 0)
        near_bias = jnp.where(4 * (row & 255) + (row >> 8) + base < length, 0.0, NEGATIVE).astype(BF)
        rq = lax.broadcasted_iota(jnp.int32, (1, ROWS), 1)
        real = jnp.where(4 * (rq & 255) + (rq >> 8) + base < length, 1.0, 0.0)
        tail = jnp.where(lax.broadcasted_iota(jnp.int32, (16, ROWS), 0) == 0, 1.0, 0.0).astype(BF)
        o = HEAD * (1 - a)
        c = 2 * lax.rem(i, 2) + a
        mine = (lane < HEAD) if a == 0 else (lane >= HEAD)
        mine_t = (sub < HEAD) if a == 0 else (sub >= HEAD)
        sl = slice(HEAD * a, HEAD * a + HEAD)
        far_bias = jnp.where(4 * row + c < length, 0.0, NEGATIVE).astype(BF)
        ones2 = jnp.where((lane == o) | (lane == o + 1), one, zero)
        ka = jnp.where(mine, k[:, lanes], jnp.where(lane == o, near_bias, zero))
        va = jnp.where(mine, v[:, lanes], ones2)
        t_scr[1] = jnp.where(mine_t, t_scr[4], jnp.where(sub == o, one, zero))
        vta = jnp.concatenate([t_scr[6, sl, :], tail], axis=0)
        own = ds(c * FAR, FAR, FAR)
        for b in (1, 2, 3):
            at = ds(lax.rem(c + b, 4) * FAR, FAR, FAR)
            s = nn(ka, t_scr[1, :, at])
            e_scr[:, at] = jnp.exp2(s - jnp.max(s, axis=0, keepdims=True)).astype(BF)
        if a == 0:
            receive(i)
        kfa = jnp.where(mine, far[:, i, 0].reshape(ROWS, 128), jnp.where(lane == o, far_bias, zero))
        vfa = jnp.where(mine, far[:, i, 1].reshape(ROWS, 128), ones2)
        qc = t_scr[1, :, own]
        sf = nn(kfa, qc)
        s = nn(ka, qc)
        peak = jnp.maximum(jnp.max(s, axis=0, keepdims=True), jnp.max(sf, axis=0, keepdims=True))
        e_scr[:, own] = jnp.exp2(s - peak).astype(BF)
        ef = jnp.exp2(sf - peak).astype(BF)
        o_scr[...] = nn(vta, e_scr[...])
        o_scr[:, own] = o_scr[:, own] + nn(jnp.concatenate([t_scr[8, sl, :], tail], axis=0), ef)
        weight = real / o_scr[HEAD : HEAD + 1]
        cx = (o_scr[:HEAD] * weight).astype(BF)
        ctxT[i, sl, :] = cx
        dob = t_scr[2, sl, :].astype(F32)
        shift = -weight * jnp.sum(cx.astype(F32) * dob, axis=0, keepdims=True)
        high = shift.astype(BF)
        low = (shift - high.astype(F32)).astype(BF)
        sub2 = lax.broadcasted_iota(jnp.int32, (HEAD, ROWS), 0)
        t_scr[0, sl, :] = (dob * weight).astype(BF)
        t_scr[0, o : o + HEAD, :] = jnp.where(sub2 == 0, high, jnp.where(sub2 == 1, low, zero))
        dwc = t_scr[0, :, own]
        dsf = ef * nn(vfa, dwc).astype(BF)
        dfk = (nt(qc[sl], dsf) * LN2).astype(BF)
        dfv = nt(dwc[sl], ef).astype(BF)
        for j in range(4):
            dfs[slot, a, j, 0] = dfk[:, j * FAR : j * FAR + FAR]
            dfs[slot, a, j, 1] = dfv[:, j * FAR : j * FAR + FAR]
        for n in (1, 2, 3):
            df_copy(i, a, n).start()
        for b in range(4):
            at = slice(b * FAR, b * FAR + FAR)
            ds_scr[:, at] = e_scr[:, at] * nn(va, t_scr[0, :, at]).astype(BF)
        o_scr[:HEAD] = nn(t_scr[5, sl, :], ds_scr[...])
        o_scr[:HEAD, own] = o_scr[:HEAD, own] + nn(t_scr[7, sl, :], dsf)
        dqT[i, sl, :] = (o_scr[:HEAD] * 0.125).astype(BF)
        near[slot, 0, sl, :] = nt(t_scr[1, sl, :], ds_scr[...]) * LN2
        near[slot, 1, sl, :] = nt(t_scr[0, sl, :], e_scr[...])

    def weigh(p):
        slot = lax.rem(p, 2)
        for a in range(2):
            for n in (1, 2, 3):
                df_copy(p, a, n).wait()
            sl = slice(HEAD * a, HEAD * a + HEAD)
            at = ds((2 * slot + a) * FAR, FAR, FAR)
            for n, dst in ((0, dkT), (1, dvT)):
                own = dfs[slot, a, y, n].astype(F32)
                for m in range(3):
                    own = own + dfr[p, a, m, n].astype(F32)
                dst[p, sl, :] = near[slot, n, sl, :].astype(BF)
                dst[p, sl, at] = (near[slot, n, sl, at] + own).astype(BF)
        for n, src in enumerate((dqT, dkT, dvT)):
            part[slot, n * D : n * D + D, :] = nt(xpT[...], src[p]).astype(BF)
        gout = nn(ctxT[p], cp[...]).astype(BF)
        for t in range(6):
            at = 3 * D + t * 128
            part[slot, at : at + 128, :] = gout[:, t * 128 : t * 128 + 128]
        a_copy(p).start()

    def sum_core(p):
        slot = lax.rem(p, 2)
        a_copy(p).wait()
        mine = part[slot, ds(core * HALF, HALF, HALF), :]
        bs[slot] = (mine.astype(F32) + ar[p].astype(F32)).astype(BF)
        to_plane(b_copy, p)

    def sum_plane(p):
        b_all(p).wait()
        acc = bs[lax.rem(p, 2), ds(spot * PIECE, PIECE, PIECE), :].astype(F32)
        for n in range(PLANE - 1):
            acc = acc + br[p, n].astype(F32)
        yr[p, y] = acc.astype(BF)
        for n in (1, 2, 3):
            y_copy(p, n, y).start()

    def sum_y(p):
        for n in (1, 2, 3):
            y_copy(p, n, y).wait_send()
            y_copy(p, n, back(y, n)).wait_recv()
        acc = yr[p, 0].astype(F32)
        for n in (1, 2, 3):
            acc = acc + yr[p, n].astype(F32)
        fin[p] = acc.astype(BF)
        gl_copy(p).start()
        to_plane(g_copy, p)

    def gather(p):
        gl_copy(p).wait()
        g_all(p).wait()
        gc_copy(p, core).start()

    def end(p):
        gc_copy(p, core).wait_send()
        gc_copy(p, 1 - core).wait_recv()

    first = ((weigh, 1), (sum_plane, 2), (gather, 3))
    second = ((sum_core, 1), (sum_y, 2), (end, 3))

    def step(i, carry):
        prepare(i)
        attend(i, 0)
        pl.when(i < PAIRS - 2)(lambda: send_far(i + 2))
        for run, lag in first:
            pl.when(i >= lag)(lambda run=run, lag=lag: run(i - lag))
        attend(i, 1)
        for run, lag in second:
            pl.when(i >= lag)(lambda run=run, lag=lag: run(i - lag))
        return carry

    lax.fori_loop(0, PAIRS, step, 0)

    place = selection(True)

    def cols(ref, j):
        return jnp.concatenate(
            [ref[:, :, c * FAR + j * 128 : c * FAR + j * 128 + 128].reshape(D, 128) for c in range(4)], axis=1
        )

    def attended(j):
        outT = nn(wo[...].T, cols(ctxT, j)).astype(BF)
        q[j * 512 : j * 512 + 512, :] = nt(place, outT).astype(BF)

    def patch_grads(j):
        gT = nn(wq[...], cols(dqT, j)) + nn(wk[...], cols(dkT, j)) + nn(wv[...], cols(dvT, j))
        k[j * 512 : j * 512 + 512, :] = nt(place, gT.astype(BF)).astype(BF)

    att_copy = pltpu.make_async_copy(q, att_hbm, out_sem.at[0])
    grad_copy = pltpu.make_async_copy(k, gx_hbm, out_sem.at[1])

    sum_plane(4)
    gather(3)
    attended(0)
    weigh(5)
    sum_y(4)
    end(3)
    attended(1)
    att_copy.start()
    sum_core(5)
    gather(4)
    patch_grads(0)
    sum_plane(5)
    end(4)
    patch_grads(1)
    grad_copy.start()
    sum_y(5)
    gather(5)
    end(5)
    att_copy.wait()
    grad_copy.wait()
    for p in range(PAIRS):
        for n in (1, 2, 3):
            far_copy(p, n, y).wait_send()


def sublayer(info, x, cot, wq, wk, wv, wo):
    anywhere = pl.BlockSpec(memory_space=pl.ANY)
    dma = pltpu.SemaphoreType.DMA
    three, each = dma((3, PAIRS)), dma((PAIRS,))
    scratch = [
        *[pltpu.VMEM((D, D), BF)] * 4,
        pltpu.VMEM((D, ROWS), BF),
        pltpu.VMEM((ROWS, D), BF),
        *[pltpu.VMEM((ROWS, D), BF)] * 4,
        pltpu.VMEM((4, PAIRS, 2, FAR, 128), BF),
        *[pltpu.VMEM((PAIRS, 128, ROWS), BF)] * 4,
        pltpu.VMEM((ROWS, ROWS), BF),
        pltpu.VMEM((ROWS, ROWS), BF),
        pltpu.VMEM((9, 128, ROWS), BF),
        pltpu.VMEM((HEAD + 16, ROWS), F32),
        pltpu.VMEM((2, 2, 128, ROWS), F32),
        pltpu.VMEM((2, 2, 4, 2, HEAD, FAR), BF),
        pltpu.VMEM((PAIRS, 2, 3, 2, HEAD, FAR), BF),
        pltpu.VMEM((2, PART, 128), BF),
        pltpu.VMEM((PAIRS, HALF, 128), BF),
        pltpu.VMEM((2, HALF, 128), BF),
        pltpu.VMEM((PAIRS, PLANE - 1, PIECE, 128), BF),
        pltpu.VMEM((PAIRS, 4, PIECE, 128), BF),
        pltpu.VMEM((PAIRS, PIECE, 128), BF),
        dma((6,)),
        three, three, dma((2, 3, PAIRS)), dma((2, 3, PAIRS)), each, each, each, each, three, three,
        each, each, each, each, each, dma((2,)),
    ]
    return pl.pallas_call(
        kernel,
        in_specs=[pl.BlockSpec(memory_space=pltpu.SMEM)] + [anywhere] * 6,
        out_specs=[anywhere] * 3,
        out_shape=[
            jax.ShapeDtypeStruct((ROWS, D), BF),
            jax.ShapeDtypeStruct((ROWS, D), BF),
            jax.ShapeDtypeStruct((PAIRS, PART, 128), BF),
        ],
        scratch_shapes=scratch,
        compiler_params=pltpu.CompilerParams(
            vmem_limit_bytes=VMEM_LIMIT, collective_id=0, has_side_effects=True
        ),
    )(info, x, cot, wq, wk, wv, wo)


def assemble_kernel(att, gx, total, att_out, gx_out, gq, gk, gv, go):
    att_out[...] = att[...]
    gx_out[...] = gx[...]
    for n, ref in enumerate((gq, gk, gv)):
        ref[...] = total[0, n * D : n * D + D, :]
    for t in range(PAIRS):
        go[:, t * 128 : t * 128 + 128] = total[0, 3 * D + t * 128 : 3 * D + t * 128 + 128, :]


def assemble(att, gx, total):
    rows, square = jax.ShapeDtypeStruct((ROWS, D), BF), jax.ShapeDtypeStruct((D, D), BF)
    wide = pl.BlockSpec((ROWS, 128), lambda p: (0, p))
    column = pl.BlockSpec((D, 128), lambda p: (0, p))
    return pl.pallas_call(
        assemble_kernel,
        grid=(PAIRS,),
        in_specs=[wide, wide, pl.BlockSpec((1, PART, 128), lambda p: (p, 0, 0))],
        out_specs=[wide, wide, column, column, column, pl.BlockSpec((128, D), lambda p: (p, 0))],
        out_shape=[rows, rows, square, square, square, square],
        compiler_params=pltpu.CompilerParams(vmem_limit_bytes=VMEM_LIMIT),
    )(att, gx, total)


def local(patches, wq, wk, wv, wo, lengths, cotangent):
    att, gx, total = sublayer(lengths, patches[0], cotangent[0], wq, wk, wv, wo)
    att, gx, *grads = assemble(att, gx, total)
    return (att[None], gx[None], *grads)


def solution(mesh):
    split = P("slide", "seq", None)
    return jax.shard_map(
        local,
        mesh=mesh,
        in_specs=(split, P(), P(), P(), P(), P("slide"), split),
        out_specs=(split, split, P(), P(), P(), P()),
        check_vma=False,
    )
```

```python
import math

import jax
import jax.numpy as jnp
from jax import lax
from jax.experimental import pallas as pl
from jax.experimental.pallas import tpu as pltpu
from jax.sharding import PartitionSpec as P

BF, F32 = jnp.bfloat16, jnp.float32
MESH = pl.DeviceIdType.MESH
NEGATIVE = -1e30
ROWS, D, HEAD, PAIRS = 1024, 768, 64, 6
FAR = 256
LN2 = math.log(2.0)
QUERY_SCALE = 1.0 / (math.sqrt(HEAD) * LN2)
VMEM_LIMIT = 62 << 20
PART, HALF, PIECE = 3072, 1536, 96
PLANE = 16
GROUPS = ((0, 2), (2, 2), (4, 1), (5, 1))


def nn(a, b):
    return lax.dot_general(a, b, (((1,), (0,)), ((), ())), preferred_element_type=F32)


def nt(a, b):
    return lax.dot_general(a, b, (((1,), (1,)), ((), ())), preferred_element_type=F32)


def selection(transposed):
    a = lax.broadcasted_iota(jnp.int32, (512, 512), 1 if transposed else 0)
    b = lax.broadcasted_iota(jnp.int32, (512, 512), 0 if transposed else 1)
    return jnp.where(4 * (a & 127) + (a >> 7) == b, 1.0, 0.0).astype(BF)


def kernel(
    info, x_hbm, cot_hbm, wq_hbm, wk_hbm, wv_hbm, wo_hbm,
    att_hbm, gx_hbm, total,
    wq, wk, wv, wo, xpT, cp, q, k, v, do, far,
    ctxT, dqT, dkT, dvT, e_scr, ds_scr, t_scr, o_scr, near,
    dfs, dfr, part, ar, bs, br, yr, fin,
    load_sem, far_s, far_r, df_s, df_r, a_s, a_r, b_s, b_r, y_s, y_r,
    g_s, g_r, gl_s, gc_s, gc_r, out_sem,
):
    y = lax.axis_index("seq").astype(jnp.int32)
    slide = lax.axis_index("slide").astype(jnp.int32)
    spot = lax.div(slide, 2)
    core = lax.rem(slide, 2)
    length = info[0]
    base = y * ROWS

    def y_peer(n):
        return (lax.rem(y + n, 4), slide)

    def plane_peer(n):
        return (y, 2 * lax.rem(spot + n, PLANE) + core)

    sibling = (y, slide + 1 - 2 * core)

    loads = [
        pltpu.make_async_copy(src, dst, load_sem.at[n])
        for n, (src, dst) in enumerate(
            (
                (x_hbm, e_scr.at[:, 0:D]),
                (wk_hbm, wk),
                (wv_hbm, wv),
                (cot_hbm, ds_scr.at[:, 0:D]),
                (wo_hbm, wo),
                (wq_hbm, wq),
            )
        )
    ]
    for copy in loads:
        copy.start()
    barrier = pltpu.get_barrier_semaphore()
    peers = [sibling] + [y_peer(n) for n in (1, 2, 3)] + [plane_peer(n) for n in range(1, PLANE)]
    for peer in peers:
        pl.semaphore_signal(barrier, inc=1, device_id=peer, device_id_type=MESH)

    def remote(src, dst, send, recv, peer):
        return pltpu.make_async_remote_copy(
            src_ref=src, dst_ref=dst, send_sem=send, recv_sem=recv, device_id=peer, device_id_type=MESH
        )

    def ds(start, size, step):
        return pl.ds(pl.multiple_of(start, step), size)

    def far_copy(p, n, src):
        return remote(far.at[src, p], far.at[src, p], far_s.at[n - 1, p], far_r.at[n - 1, p], y_peer(n))

    def df_copy(p, n):
        block = dfs.at[lax.rem(p, 2), lax.rem(y + n, 4)]
        return remote(block, dfr.at[p, n - 1], df_s.at[n - 1, p], df_r.at[n - 1, p], y_peer(n))

    def span(g):
        return slice(GROUPS[g][0], sum(GROUPS[g]))

    def a_copy(g):
        block = part.at[span(g), ds((1 - core) * HALF, HALF, HALF)]
        return remote(block, ar.at[span(g)], a_s.at[g], a_r.at[g], sibling)

    def b_copy(g, n):
        block = bs.at[span(g), ds(lax.rem(spot + n, PLANE) * PIECE, PIECE, PIECE)]
        return remote(block, br.at[n - 1, span(g)], b_s.at[g], b_r.at[g], plane_peer(n))

    def b_all(g):
        block = br.at[:, span(g)]
        return remote(block, block, b_s.at[g], b_r.at[g], sibling)

    def y_copy(g, n, src):
        block = yr.at[src, span(g)]
        return remote(block, block, y_s.at[n - 1, g], y_r.at[n - 1, g], y_peer(n))

    def g_copy(g, n):
        block = total.at[span(g), ds(core * HALF + spot * PIECE, PIECE, PIECE)]
        return remote(fin.at[span(g)], block, g_s.at[g], g_r.at[g], plane_peer(n))

    def g_all(g):
        block = total.at[span(g), 0 : HALF - PIECE]
        return remote(block, block, g_s.at[g], g_r.at[g], sibling)

    def gl_copy(g):
        block = total.at[span(g), ds(core * HALF + spot * PIECE, PIECE, PIECE)]
        return pltpu.make_async_copy(fin.at[span(g)], block, gl_s.at[g])

    def gc_copy(g, src):
        block = total.at[span(g), ds(src * HALF, HALF, HALF)]
        return remote(block, block, gc_s.at[g], gc_r.at[g], sibling)

    def to_plane(copy, g):
        def one(n, carry):
            copy(g, n).start()
            return carry

        lax.fori_loop(1, PLANE, one, 0)

    def back(index, n):
        return lax.rem(index + 4 - n, 4)

    def send_far(p):
        for n in (1, 2, 3):
            far_copy(p, n, y).start()

    pick = selection(False)
    left = lax.broadcasted_iota(jnp.int32, (128, 128), 1) < HEAD

    def spread(ref, j, value):
        for c in range(4):
            ref[c * FAR + j * 128 : c * FAR + j * 128 + 128, :] = value[c * 128 : c * 128 + 128]

    loads[0].wait()
    loads[1].wait()
    loads[2].wait()
    rows = []
    for j in range(2):
        block = nn(pick, e_scr[j * 512 : j * 512 + 512, 0:D]).astype(BF)
        rows.append(block)
        for n, (w, ref) in enumerate(((wk, k), (wv, v))):
            value = nn(block, w[...]).astype(BF)
            spread(ref, j, value)
            for t in range(PAIRS):
                c = 256 * (t % 2)
                at = slice(t * 128, t * 128 + 128)
                far[y, t, n, j * 128 : j * 128 + 128, :] = jnp.where(
                    left, value[c : c + 128, at], value[c + 128 : c + 256, at]
                )
    pl.semaphore_wait(barrier, len(peers))
    send_far(0)
    loads[3].wait()
    loads[4].wait()
    loads[5].wait()
    for j in range(2):
        spread(q, j, (nn(rows[j], wq[...]) * QUERY_SCALE).astype(BF))
        blockT = rows[j].T
        for c in range(4):
            xpT[:, c * FAR + j * 128 : c * FAR + j * 128 + 128] = blockT[:, c * 128 : c * 128 + 128]
        block = nn(pick, ds_scr[j * 512 : j * 512 + 512, 0:D]).astype(BF)
        spread(cp, j, block)
        spread(do, j, nt(block, wo[...]).astype(BF))

    send_far(1)
    zero, one = jnp.zeros((), BF), jnp.ones((), BF)

    def prepare(i):
        at = ds(i * 128, 128, 128)
        t_scr[2] = do[:, at].T
        t_scr[4] = q[:, at].T
        t_scr[5] = k[:, at].T
        t_scr[6] = v[:, at].T

    def receive(i):
        for n in (1, 2, 3):
            far_copy(i, n, back(y, n)).wait_recv()
        for s in range(4):
            t_scr[7, :, s * FAR : s * FAR + FAR] = far[s, i, 0].T
            t_scr[8, :, s * FAR : s * FAR + FAR] = far[s, i, 1].T

    def attend(i, a):
        slot = lax.rem(i, 2)
        lanes = ds(i * 128, 128, 128)
        lane = lax.broadcasted_iota(jnp.int32, (ROWS, 128), 1)
        row = lax.broadcasted_iota(jnp.int32, (ROWS, 128), 0)
        sub = lax.broadcasted_iota(jnp.int32, (128, ROWS), 0)
        near_bias = jnp.where(4 * (row & 255) + (row >> 8) + base < length, 0.0, NEGATIVE).astype(BF)
        rq = lax.broadcasted_iota(jnp.int32, (1, ROWS), 1)
        real = jnp.where(4 * (rq & 255) + (rq >> 8) + base < length, 1.0, 0.0)
        tail = jnp.where(lax.broadcasted_iota(jnp.int32, (16, ROWS), 0) == 0, 1.0, 0.0).astype(BF)
        o = HEAD * (1 - a)
        c = 2 * lax.rem(i, 2) + a
        mine = (lane < HEAD) if a == 0 else (lane >= HEAD)
        mine_t = (sub < HEAD) if a == 0 else (sub >= HEAD)
        sl = slice(HEAD * a, HEAD * a + HEAD)
        far_bias = jnp.where(4 * row + c < length, 0.0, NEGATIVE).astype(BF)
        ones2 = jnp.where((lane == o) | (lane == o + 1), one, zero)
        ka = jnp.where(mine, k[:, lanes], jnp.where(lane == o, near_bias, zero))
        va = jnp.where(mine, v[:, lanes], ones2)
        t_scr[1] = jnp.where(mine_t, t_scr[4], jnp.where(sub == o, one, zero))
        vta = jnp.concatenate([t_scr[6, sl, :], tail], axis=0)
        own = ds(c * FAR, FAR, FAR)
        for b in (1, 2, 3):
            at = ds(lax.rem(c + b, 4) * FAR, FAR, FAR)
            s = nn(ka, t_scr[1, :, at])
            e_scr[:, at] = jnp.exp2(s - jnp.max(s, axis=0, keepdims=True)).astype(BF)
        if a == 0:
            receive(i)
        kfa = jnp.where(mine, far[:, i, 0].reshape(ROWS, 128), jnp.where(lane == o, far_bias, zero))
        vfa = jnp.where(mine, far[:, i, 1].reshape(ROWS, 128), ones2)
        qc = t_scr[1, :, own]
        sf = nn(kfa, qc)
        s = nn(ka, qc)
        peak = jnp.maximum(jnp.max(s, axis=0, keepdims=True), jnp.max(sf, axis=0, keepdims=True))
        e_scr[:, own] = jnp.exp2(s - peak).astype(BF)
        ef = jnp.exp2(sf - peak).astype(BF)
        o_scr[...] = nn(vta, e_scr[...])
        o_scr[:, own] = o_scr[:, own] + nn(jnp.concatenate([t_scr[8, sl, :], tail], axis=0), ef)
        weight = real / o_scr[HEAD : HEAD + 1]
        cx = (o_scr[:HEAD] * weight).astype(BF)
        ctxT[i, sl, :] = cx
        dob = t_scr[2, sl, :].astype(F32)
        shift = -weight * jnp.sum(cx.astype(F32) * dob, axis=0, keepdims=True)
        high = shift.astype(BF)
        low = (shift - high.astype(F32)).astype(BF)
        sub2 = lax.broadcasted_iota(jnp.int32, (HEAD, ROWS), 0)
        t_scr[0, sl, :] = (dob * weight).astype(BF)
        t_scr[0, o : o + HEAD, :] = jnp.where(sub2 == 0, high, jnp.where(sub2 == 1, low, zero))
        dwc = t_scr[0, :, own]
        dsf = ef * nn(vfa, dwc).astype(BF)
        dfk = (nt(qc[sl], dsf) * LN2).astype(BF)
        dfv = nt(dwc[sl], ef).astype(BF)
        for j in range(4):
            dfs[slot, j, a, 0] = dfk[:, j * FAR : j * FAR + FAR]
            dfs[slot, j, a, 1] = dfv[:, j * FAR : j * FAR + FAR]
        if a == 1:
            for n in (1, 2, 3):
                df_copy(i, n).start()
        for b in range(4):
            at = slice(b * FAR, b * FAR + FAR)
            ds_scr[:, at] = e_scr[:, at] * nn(va, t_scr[0, :, at]).astype(BF)
        o_scr[:HEAD] = nn(t_scr[5, sl, :], ds_scr[...])
        o_scr[:HEAD, own] = o_scr[:HEAD, own] + nn(t_scr[7, sl, :], dsf)
        dqT[i, sl, :] = (o_scr[:HEAD] * 0.125).astype(BF)
        near[slot, 0, sl, :] = nt(t_scr[1, sl, :], ds_scr[...]) * LN2
        near[slot, 1, sl, :] = nt(t_scr[0, sl, :], e_scr[...])

    def weigh(p):
        slot = lax.rem(p, 2)
        for n in (1, 2, 3):
            df_copy(p, n).wait()
        for a in range(2):
            sl = slice(HEAD * a, HEAD * a + HEAD)
            at = ds((2 * slot + a) * FAR, FAR, FAR)
            for n, dst in ((0, dkT), (1, dvT)):
                own = dfs[slot, y, a, n].astype(F32)
                for m in range(3):
                    own = own + dfr[p, m, a, n].astype(F32)
                dst[p, sl, :] = near[slot, n, sl, :].astype(BF)
                dst[p, sl, at] = (near[slot, n, sl, at] + own).astype(BF)
        for n, src in enumerate((dqT, dkT, dvT)):
            part[p, n * D : n * D + D, :] = nt(xpT[...], src[p]).astype(BF)
        gout = nn(ctxT[p], cp[...]).astype(BF)
        for t in range(6):
            at = 3 * D + t * 128
            part[p, at : at + 128, :] = gout[:, t * 128 : t * 128 + 128]

    def send(g):
        a_copy(g).start()

    def sum_core(g):
        a_copy(g).wait()
        for p in range(PAIRS)[span(g)]:
            mine = part[p, ds(core * HALF, HALF, HALF), :]
            bs[p] = (mine.astype(F32) + ar[p].astype(F32)).astype(BF)
        to_plane(b_copy, g)

    def sum_plane(g):
        b_all(g).wait()
        for p in range(PAIRS)[span(g)]:
            acc = bs[p, ds(spot * PIECE, PIECE, PIECE), :].astype(F32)
            for n in range(PLANE - 1):
                acc = acc + br[n, p].astype(F32)
            yr[y, p] = acc.astype(BF)
        for n in (1, 2, 3):
            y_copy(g, n, y).start()

    def sum_y(g):
        for n in (1, 2, 3):
            y_copy(g, n, y).wait_send()
            y_copy(g, n, back(y, n)).wait_recv()
        acc = yr[0, span(g)].astype(F32)
        for n in (1, 2, 3):
            acc = acc + yr[n, span(g)].astype(F32)
        fin[span(g)] = acc.astype(BF)
        gl_copy(g).start()
        to_plane(g_copy, g)

    def gather(g):
        gl_copy(g).wait()
        g_all(g).wait()
        gc_copy(g, core).start()

    def end(g):
        gc_copy(g, core).wait_send()
        gc_copy(g, 1 - core).wait_recv()

    first = ((2, send, 0), (4, sum_y, 0), (4, send, 1), (5, send, 2), (5, gather, 0))
    second = ((2, sum_core, 0), (3, sum_plane, 0), (4, sum_core, 1), (5, sum_plane, 1), (5, sum_core, 2))

    def step(i, carry):
        prepare(i)
        attend(i, 0)
        pl.when(i < PAIRS - 2)(lambda: send_far(i + 2))
        pl.when(i > 0)(lambda: weigh(i - 1))
        for when, run, g in first:
            pl.when(i == when)(lambda run=run, g=g: run(g))
        attend(i, 1)
        for when, run, g in second:
            pl.when(i == when)(lambda run=run, g=g: run(g))
        return carry

    lax.fori_loop(0, PAIRS, step, 0)

    place = selection(True)

    def cols(ref, j):
        return jnp.concatenate(
            [ref[:, :, c * FAR + j * 128 : c * FAR + j * 128 + 128].reshape(D, 128) for c in range(4)], axis=1
        )

    def attended(j):
        outT = nn(wo[...].T, cols(ctxT, j)).astype(BF)
        q[j * 512 : j * 512 + 512, :] = nt(place, outT).astype(BF)

    def patch_grads(j):
        gT = nn(wq[...], cols(dqT, j)) + nn(wk[...], cols(dkT, j)) + nn(wv[...], cols(dvT, j))
        k[j * 512 : j * 512 + 512, :] = nt(place, gT.astype(BF)).astype(BF)

    att_copy = pltpu.make_async_copy(q, att_hbm, out_sem.at[0])
    grad_copy = pltpu.make_async_copy(k, gx_hbm, out_sem.at[1])

    attended(0)
    weigh(PAIRS - 1)
    send(3)
    sum_y(1)
    attended(1)
    att_copy.start()
    sum_core(3)
    sum_plane(2)
    patch_grads(0)
    sum_plane(3)
    sum_y(2)
    gather(1)
    patch_grads(1)
    grad_copy.start()
    sum_y(3)
    gather(2)
    end(0)
    end(1)
    gather(3)
    end(2)
    end(3)
    att_copy.wait()
    grad_copy.wait()
    for p in range(PAIRS):
        for n in (1, 2, 3):
            far_copy(p, n, y).wait_send()


def sublayer(info, x, cot, wq, wk, wv, wo):
    anywhere = pl.BlockSpec(memory_space=pl.ANY)
    dma = pltpu.SemaphoreType.DMA
    three, each, group = dma((3, PAIRS)), dma((len(GROUPS),)), dma((3, len(GROUPS)))
    scratch = [
        *[pltpu.VMEM((D, D), BF)] * 4,
        pltpu.VMEM((D, ROWS), BF),
        pltpu.VMEM((ROWS, D), BF),
        *[pltpu.VMEM((ROWS, D), BF)] * 4,
        pltpu.VMEM((4, PAIRS, 2, FAR, 128), BF),
        *[pltpu.VMEM((PAIRS, 128, ROWS), BF)] * 4,
        pltpu.VMEM((ROWS, ROWS), BF),
        pltpu.VMEM((ROWS, ROWS), BF),
        pltpu.VMEM((9, 128, ROWS), BF),
        pltpu.VMEM((HEAD + 16, ROWS), F32),
        pltpu.VMEM((2, 2, 128, ROWS), F32),
        pltpu.VMEM((2, 4, 2, 2, HEAD, FAR), BF),
        pltpu.VMEM((PAIRS, 3, 2, 2, HEAD, FAR), BF),
        pltpu.VMEM((PAIRS, PART, 128), BF),
        pltpu.VMEM((PAIRS, HALF, 128), BF),
        pltpu.VMEM((PAIRS, HALF, 128), BF),
        pltpu.VMEM((PLANE - 1, PAIRS, PIECE, 128), BF),
        pltpu.VMEM((4, PAIRS, PIECE, 128), BF),
        pltpu.VMEM((PAIRS, PIECE, 128), BF),
        dma((6,)),
        three, three, three, three, each, each, each, each, group, group,
        each, each, each, each, each, dma((2,)),
    ]
    return pl.pallas_call(
        kernel,
        in_specs=[pl.BlockSpec(memory_space=pltpu.SMEM)] + [anywhere] * 6,
        out_specs=[anywhere] * 3,
        out_shape=[
            jax.ShapeDtypeStruct((ROWS, D), BF),
            jax.ShapeDtypeStruct((ROWS, D), BF),
            jax.ShapeDtypeStruct((PAIRS, PART, 128), BF),
        ],
        scratch_shapes=scratch,
        compiler_params=pltpu.CompilerParams(
            vmem_limit_bytes=VMEM_LIMIT, collective_id=0, has_side_effects=True
        ),
    )(info, x, cot, wq, wk, wv, wo)


def assemble_kernel(att, gx, total, att_out, gx_out, gq, gk, gv, go):
    att_out[...] = att[...]
    gx_out[...] = gx[...]
    for p in range(2):
        at = slice(p * 128, p * 128 + 128)
        for n, ref in enumerate((gq, gk, gv)):
            ref[:, at] = total[p, n * D : n * D + D, :]
        for t in range(PAIRS):
            go[at, t * 128 : t * 128 + 128] = total[p, 3 * D + t * 128 : 3 * D + t * 128 + 128, :]


def assemble(att, gx, total):
    rows, square = jax.ShapeDtypeStruct((ROWS, D), BF), jax.ShapeDtypeStruct((D, D), BF)
    wide = pl.BlockSpec((ROWS, 256), lambda p: (0, p))
    column = pl.BlockSpec((D, 256), lambda p: (0, p))
    return pl.pallas_call(
        assemble_kernel,
        grid=(PAIRS // 2,),
        in_specs=[wide, wide, pl.BlockSpec((2, PART, 128), lambda p: (p, 0, 0))],
        out_specs=[wide, wide, column, column, column, pl.BlockSpec((256, D), lambda p: (p, 0))],
        out_shape=[rows, rows, square, square, square, square],
        compiler_params=pltpu.CompilerParams(vmem_limit_bytes=VMEM_LIMIT),
    )(att, gx, total)


def local(patches, wq, wk, wv, wo, lengths, cotangent):
    att, gx, total = sublayer(lengths, patches[0], cotangent[0], wq, wk, wv, wo)
    att, gx, *grads = assemble(att, gx, total)
    return (att[None], gx[None], *grads)


def solution(mesh):
    split = P("slide", "seq", None)
    return jax.shard_map(
        local,
        mesh=mesh,
        in_specs=(split, P(), P(), P(), P(), P("slide"), split),
        out_specs=(split, split, P(), P(), P(), P()),
        check_vma=False,
    )
```

```python
import math

import jax
import jax.numpy as jnp
from jax import lax
from jax.experimental import pallas as pl
from jax.experimental.pallas import tpu as pltpu
from jax.sharding import PartitionSpec as P

BF, F32 = jnp.bfloat16, jnp.float32
MESH = pl.DeviceIdType.MESH
NEGATIVE = -1e30
ROWS, D, HEAD, PAIRS = 1024, 768, 64, 6
FAR = 256
LN2 = math.log(2.0)
QUERY_SCALE = 1.0 / (math.sqrt(HEAD) * LN2)
VMEM_LIMIT = 62 << 20
PART, HALF, PIECE = 3072, 1536, 96
PLANE = 16
GROUPS = ((0, 2), (2, 2), (4, 1), (5, 1))


def nn(a, b):
    return lax.dot_general(a, b, (((1,), (0,)), ((), ())), preferred_element_type=F32)


def nt(a, b):
    return lax.dot_general(a, b, (((1,), (1,)), ((), ())), preferred_element_type=F32)


def selection(transposed):
    a = lax.broadcasted_iota(jnp.int32, (512, 512), 1 if transposed else 0)
    b = lax.broadcasted_iota(jnp.int32, (512, 512), 0 if transposed else 1)
    return jnp.where(4 * (a & 127) + (a >> 7) == b, 1.0, 0.0).astype(BF)


def kernel(
    info, x_hbm, cot_hbm, wq_hbm, wk_hbm, wv_hbm, wo_hbm,
    att_hbm, gx_hbm, total,
    wq, wk, wv, wo, xpT, cp, q, k, v, do, far,
    ctxT, dqT, dkT, dvT, e_scr, ds_scr, t_scr, o_scr, near,
    dfs, dfr, part, ar, bs, br, yr, fin,
    load_sem, far_s, far_r, df_s, df_r, a_s, a_r, b_s, b_r, y_s, y_r,
    g_s, g_r, gl_s, gc_s, gc_r, out_sem,
):
    y = lax.axis_index("seq").astype(jnp.int32)
    slide = lax.axis_index("slide").astype(jnp.int32)
    spot = lax.div(slide, 2)
    core = lax.rem(slide, 2)
    length = info[0]
    base = y * ROWS

    def y_peer(n):
        return (lax.rem(y + n, 4), slide)

    def plane_peer(n):
        return (y, 2 * lax.rem(spot + n, PLANE) + core)

    sibling = (y, slide + 1 - 2 * core)

    loads = [
        pltpu.make_async_copy(src, dst, load_sem.at[n])
        for n, (src, dst) in enumerate(
            (
                (x_hbm, e_scr.at[:, 0:D]),
                (wk_hbm, wk),
                (wv_hbm, wv),
                (cot_hbm, ds_scr.at[:, 0:D]),
                (wo_hbm, wo),
                (wq_hbm, wq),
            )
        )
    ]
    for copy in loads:
        copy.start()
    barrier = pltpu.get_barrier_semaphore()
    peers = [sibling] + [y_peer(n) for n in (1, 2, 3)] + [plane_peer(n) for n in range(1, PLANE)]
    for peer in peers:
        pl.semaphore_signal(barrier, inc=1, device_id=peer, device_id_type=MESH)

    def remote(src, dst, send, recv, peer):
        return pltpu.make_async_remote_copy(
            src_ref=src, dst_ref=dst, send_sem=send, recv_sem=recv, device_id=peer, device_id_type=MESH
        )

    def ds(start, size, step):
        return pl.ds(pl.multiple_of(start, step), size)

    def far_copy(p, n, src):
        return remote(far.at[src, p], far.at[src, p], far_s.at[n - 1, p], far_r.at[n - 1, p], y_peer(n))

    def df_copy(p, n):
        block = dfs.at[lax.rem(p, 2), lax.rem(y + n, 4)]
        return remote(block, dfr.at[p, n - 1], df_s.at[n - 1, p], df_r.at[n - 1, p], y_peer(n))

    def span(g):
        return slice(GROUPS[g][0], sum(GROUPS[g]))

    def a_copy(g):
        block = part.at[span(g), ds((1 - core) * HALF, HALF, HALF)]
        return remote(block, ar.at[span(g)], a_s.at[g], a_r.at[g], sibling)

    def b_copy(g, n):
        block = bs.at[span(g), ds(lax.rem(spot + n, PLANE) * PIECE, PIECE, PIECE)]
        return remote(block, br.at[n - 1, span(g)], b_s.at[g], b_r.at[g], plane_peer(n))

    def b_all(g):
        block = br.at[:, span(g)]
        return remote(block, block, b_s.at[g], b_r.at[g], sibling)

    def y_copy(g, n, src):
        block = yr.at[src, span(g)]
        return remote(block, block, y_s.at[n - 1, g], y_r.at[n - 1, g], y_peer(n))

    def g_copy(g, n):
        block = total.at[span(g), ds(core * HALF + spot * PIECE, PIECE, PIECE)]
        return remote(fin.at[span(g)], block, g_s.at[g], g_r.at[g], plane_peer(n))

    def g_all(g):
        block = total.at[span(g), 0 : HALF - PIECE]
        return remote(block, block, g_s.at[g], g_r.at[g], sibling)

    def gl_copy(g):
        block = total.at[span(g), ds(core * HALF + spot * PIECE, PIECE, PIECE)]
        return pltpu.make_async_copy(fin.at[span(g)], block, gl_s.at[g])

    def gc_copy(g, src):
        block = total.at[span(g), ds(src * HALF, HALF, HALF)]
        return remote(block, block, gc_s.at[g], gc_r.at[g], sibling)

    def to_plane(copy, g):
        for n in range(1, PLANE):
            copy(g, n).start()

    def back(index, n):
        return lax.rem(index + 4 - n, 4)

    def send_far(p):
        for n in (1, 2, 3):
            far_copy(p, n, y).start()

    pick = selection(False)
    left = lax.broadcasted_iota(jnp.int32, (128, 128), 1) < HEAD

    def spread(ref, j, value):
        for c in range(4):
            ref[c * FAR + j * 128 : c * FAR + j * 128 + 128, :] = value[c * 128 : c * 128 + 128]

    loads[0].wait()
    loads[1].wait()
    loads[2].wait()
    rows = []
    for j in range(2):
        block = nn(pick, e_scr[j * 512 : j * 512 + 512, 0:D]).astype(BF)
        rows.append(block)
        for n, (w, ref) in enumerate(((wk, k), (wv, v))):
            value = nn(block, w[...]).astype(BF)
            spread(ref, j, value)
            for t in range(PAIRS):
                c = 256 * (t % 2)
                at = slice(t * 128, t * 128 + 128)
                far[y, t, n, j * 128 : j * 128 + 128, :] = jnp.where(
                    left, value[c : c + 128, at], value[c + 128 : c + 256, at]
                )
    pl.semaphore_wait(barrier, len(peers))
    send_far(0)
    loads[3].wait()
    loads[4].wait()
    loads[5].wait()
    for j in range(2):
        spread(q, j, (nn(rows[j], wq[...]) * QUERY_SCALE).astype(BF))
        blockT = rows[j].T
        for c in range(4):
            xpT[:, c * FAR + j * 128 : c * FAR + j * 128 + 128] = blockT[:, c * 128 : c * 128 + 128]
        block = nn(pick, ds_scr[j * 512 : j * 512 + 512, 0:D]).astype(BF)
        spread(cp, j, block)
        spread(do, j, nt(block, wo[...]).astype(BF))

    send_far(1)
    zero, one = jnp.zeros((), BF), jnp.ones((), BF)

    def prepare(i):
        at = ds(i * 128, 128, 128)
        t_scr[2] = do[:, at].T
        t_scr[4] = q[:, at].T
        t_scr[5] = k[:, at].T
        t_scr[6] = v[:, at].T

    def receive(i):
        for n in (1, 2, 3):
            far_copy(i, n, back(y, n)).wait_recv()
        for s in range(4):
            t_scr[7, :, s * FAR : s * FAR + FAR] = far[s, i, 0].T
            t_scr[8, :, s * FAR : s * FAR + FAR] = far[s, i, 1].T

    def attend(i, a):
        slot = lax.rem(i, 2)
        lanes = ds(i * 128, 128, 128)
        lane = lax.broadcasted_iota(jnp.int32, (ROWS, 128), 1)
        row = lax.broadcasted_iota(jnp.int32, (ROWS, 128), 0)
        sub = lax.broadcasted_iota(jnp.int32, (128, ROWS), 0)
        near_bias = jnp.where(4 * (row & 255) + (row >> 8) + base < length, 0.0, NEGATIVE).astype(BF)
        rq = lax.broadcasted_iota(jnp.int32, (1, ROWS), 1)
        real = jnp.where(4 * (rq & 255) + (rq >> 8) + base < length, 1.0, 0.0)
        tail = jnp.where(lax.broadcasted_iota(jnp.int32, (16, ROWS), 0) == 0, 1.0, 0.0).astype(BF)
        o = HEAD * (1 - a)
        c = 2 * lax.rem(i, 2) + a
        mine = (lane < HEAD) if a == 0 else (lane >= HEAD)
        mine_t = (sub < HEAD) if a == 0 else (sub >= HEAD)
        sl = slice(HEAD * a, HEAD * a + HEAD)
        far_bias = jnp.where(4 * row + c < length, 0.0, NEGATIVE).astype(BF)
        ones2 = jnp.where((lane == o) | (lane == o + 1), one, zero)
        ka = jnp.where(mine, k[:, lanes], jnp.where(lane == o, near_bias, zero))
        va = jnp.where(mine, v[:, lanes], ones2)
        t_scr[1] = jnp.where(mine_t, t_scr[4], jnp.where(sub == o, one, zero))
        vta = jnp.concatenate([t_scr[6, sl, :], tail], axis=0)
        own = ds(c * FAR, FAR, FAR)
        for b in (1, 2, 3):
            at = ds(lax.rem(c + b, 4) * FAR, FAR, FAR)
            s = nn(ka, t_scr[1, :, at])
            e_scr[:, at] = jnp.exp2(s - jnp.max(s, axis=0, keepdims=True)).astype(BF)
        if a == 0:
            receive(i)
        kfa = jnp.where(mine, far[:, i, 0].reshape(ROWS, 128), jnp.where(lane == o, far_bias, zero))
        vfa = jnp.where(mine, far[:, i, 1].reshape(ROWS, 128), ones2)
        qc = t_scr[1, :, own]
        sf = nn(kfa, qc)
        s = nn(ka, qc)
        peak = jnp.maximum(jnp.max(s, axis=0, keepdims=True), jnp.max(sf, axis=0, keepdims=True))
        e_scr[:, own] = jnp.exp2(s - peak).astype(BF)
        ef = jnp.exp2(sf - peak).astype(BF)
        o_scr[...] = nn(vta, e_scr[...])
        o_scr[:, own] = o_scr[:, own] + nn(jnp.concatenate([t_scr[8, sl, :], tail], axis=0), ef)
        weight = real / o_scr[HEAD : HEAD + 1]
        cx = (o_scr[:HEAD] * weight).astype(BF)
        ctxT[i, sl, :] = cx
        dob = t_scr[2, sl, :].astype(F32)
        shift = -weight * jnp.sum(cx.astype(F32) * dob, axis=0, keepdims=True)
        high = shift.astype(BF)
        low = (shift - high.astype(F32)).astype(BF)
        sub2 = lax.broadcasted_iota(jnp.int32, (HEAD, ROWS), 0)
        t_scr[0, sl, :] = (dob * weight).astype(BF)
        t_scr[0, o : o + HEAD, :] = jnp.where(sub2 == 0, high, jnp.where(sub2 == 1, low, zero))
        dwc = t_scr[0, :, own]
        dsf = ef * nn(vfa, dwc).astype(BF)
        dfk = (nt(qc[sl], dsf) * LN2).astype(BF)
        dfv = nt(dwc[sl], ef).astype(BF)
        for j in range(4):
            dfs[slot, j, a, 0] = dfk[:, j * FAR : j * FAR + FAR]
            dfs[slot, j, a, 1] = dfv[:, j * FAR : j * FAR + FAR]
        if a == 1:
            for n in (1, 2, 3):
                df_copy(i, n).start()
        for b in range(4):
            at = slice(b * FAR, b * FAR + FAR)
            ds_scr[:, at] = e_scr[:, at] * nn(va, t_scr[0, :, at]).astype(BF)
        o_scr[:HEAD] = nn(t_scr[5, sl, :], ds_scr[...])
        o_scr[:HEAD, own] = o_scr[:HEAD, own] + nn(t_scr[7, sl, :], dsf)
        dqT[i, sl, :] = (o_scr[:HEAD] * 0.125).astype(BF)
        near[slot, 0, sl, :] = nt(t_scr[1, sl, :], ds_scr[...]) * LN2
        near[slot, 1, sl, :] = nt(t_scr[0, sl, :], e_scr[...])

    def weigh(p):
        slot = lax.rem(p, 2)
        part[p, 0:D, :] = nt(xpT[...], dqT[p]).astype(BF)
        gout = nn(ctxT[p], cp[...]).astype(BF)
        for t in range(6):
            at = 3 * D + t * 128
            part[p, at : at + 128, :] = gout[:, t * 128 : t * 128 + 128]
        for n in (1, 2, 3):
            df_copy(p, n).wait()
        for a in range(2):
            sl = slice(HEAD * a, HEAD * a + HEAD)
            at = ds((2 * slot + a) * FAR, FAR, FAR)
            for n, dst in ((0, dkT), (1, dvT)):
                own = dfs[slot, y, a, n].astype(F32)
                for m in range(3):
                    own = own + dfr[p, m, a, n].astype(F32)
                dst[p, sl, :] = near[slot, n, sl, :].astype(BF)
                dst[p, sl, at] = (near[slot, n, sl, at] + own).astype(BF)
        for n, src in ((1, dkT), (2, dvT)):
            part[p, n * D : n * D + D, :] = nt(xpT[...], src[p]).astype(BF)

    def send(g):
        a_copy(g).start()

    def sum_core(g):
        a_copy(g).wait()
        for p in range(PAIRS)[span(g)]:
            mine = part[p, ds(core * HALF, HALF, HALF), :]
            bs[p] = (mine.astype(F32) + ar[p].astype(F32)).astype(BF)
        to_plane(b_copy, g)

    def sum_plane(g):
        b_all(g).wait()
        for p in range(PAIRS)[span(g)]:
            acc = bs[p, ds(spot * PIECE, PIECE, PIECE), :].astype(F32)
            for n in range(PLANE - 1):
                acc = acc + br[n, p].astype(F32)
            yr[y, p] = acc.astype(BF)
        for n in (1, 2, 3):
            y_copy(g, n, y).start()

    def sum_y(g):
        for n in (1, 2, 3):
            y_copy(g, n, y).wait_send()
            y_copy(g, n, back(y, n)).wait_recv()
        acc = yr[0, span(g)].astype(F32)
        for n in (1, 2, 3):
            acc = acc + yr[n, span(g)].astype(F32)
        fin[span(g)] = acc.astype(BF)
        gl_copy(g).start()
        to_plane(g_copy, g)

    def gather(g):
        gl_copy(g).wait()
        g_all(g).wait()
        gc_copy(g, core).start()

    def end(g):
        gc_copy(g, core).wait_send()
        gc_copy(g, 1 - core).wait_recv()

    first = ((2, send, 0), (4, sum_y, 0), (4, send, 1), (5, send, 2), (5, gather, 0))
    second = ((2, sum_core, 0), (3, sum_plane, 0), (4, sum_core, 1), (5, sum_plane, 1), (5, sum_core, 2))

    def step(i, carry):
        prepare(i)
        attend(i, 0)
        pl.when(i < PAIRS - 2)(lambda: send_far(i + 2))
        pl.when(i > 0)(lambda: weigh(i - 1))
        for when, run, g in first:
            pl.when(i == when)(lambda run=run, g=g: run(g))
        attend(i, 1)
        for when, run, g in second:
            pl.when(i == when)(lambda run=run, g=g: run(g))
        return carry

    lax.fori_loop(0, PAIRS, step, 0)

    place = selection(True)

    def cols(ref, j):
        return jnp.concatenate(
            [ref[:, :, c * FAR + j * 128 : c * FAR + j * 128 + 128].reshape(D, 128) for c in range(4)], axis=1
        )

    def attended(j):
        outT = nn(wo[...].T, cols(ctxT, j)).astype(BF)
        q[j * 512 : j * 512 + 512, :] = nt(place, outT).astype(BF)

    def patch_grads(j):
        gT = nn(wq[...], cols(dqT, j)) + nn(wk[...], cols(dkT, j)) + nn(wv[...], cols(dvT, j))
        k[j * 512 : j * 512 + 512, :] = nt(place, gT.astype(BF)).astype(BF)

    att_copy = pltpu.make_async_copy(q, att_hbm, out_sem.at[0])
    grad_copy = pltpu.make_async_copy(k, gx_hbm, out_sem.at[1])

    attended(0)
    weigh(PAIRS - 1)
    send(3)
    sum_y(1)
    attended(1)
    att_copy.start()
    sum_core(3)
    sum_plane(2)
    patch_grads(0)
    sum_plane(3)
    sum_y(2)
    gather(1)
    patch_grads(1)
    grad_copy.start()
    sum_y(3)
    gather(2)
    end(0)
    end(1)
    gather(3)
    end(2)
    end(3)
    att_copy.wait()
    grad_copy.wait()
    for p in range(PAIRS):
        for n in (1, 2, 3):
            far_copy(p, n, y).wait_send()


def sublayer(info, x, cot, wq, wk, wv, wo):
    anywhere = pl.BlockSpec(memory_space=pl.ANY)
    dma = pltpu.SemaphoreType.DMA
    three, each, group = dma((3, PAIRS)), dma((len(GROUPS),)), dma((3, len(GROUPS)))
    scratch = [
        *[pltpu.VMEM((D, D), BF)] * 4,
        pltpu.VMEM((D, ROWS), BF),
        pltpu.VMEM((ROWS, D), BF),
        *[pltpu.VMEM((ROWS, D), BF)] * 4,
        pltpu.VMEM((4, PAIRS, 2, FAR, 128), BF),
        *[pltpu.VMEM((PAIRS, 128, ROWS), BF)] * 4,
        pltpu.VMEM((ROWS, ROWS), BF),
        pltpu.VMEM((ROWS, ROWS), BF),
        pltpu.VMEM((9, 128, ROWS), BF),
        pltpu.VMEM((HEAD + 16, ROWS), F32),
        pltpu.VMEM((2, 2, 128, ROWS), F32),
        pltpu.VMEM((2, 4, 2, 2, HEAD, FAR), BF),
        pltpu.VMEM((PAIRS, 3, 2, 2, HEAD, FAR), BF),
        pltpu.VMEM((PAIRS, PART, 128), BF),
        pltpu.VMEM((PAIRS, HALF, 128), BF),
        pltpu.VMEM((PAIRS, HALF, 128), BF),
        pltpu.VMEM((PLANE - 1, PAIRS, PIECE, 128), BF),
        pltpu.VMEM((4, PAIRS, PIECE, 128), BF),
        pltpu.VMEM((PAIRS, PIECE, 128), BF),
        dma((6,)),
        three, three, three, three, each, each, each, each, group, group,
        each, each, each, each, each, dma((2,)),
    ]
    return pl.pallas_call(
        kernel,
        in_specs=[pl.BlockSpec(memory_space=pltpu.SMEM)] + [anywhere] * 6,
        out_specs=[anywhere] * 3,
        out_shape=[
            jax.ShapeDtypeStruct((ROWS, D), BF),
            jax.ShapeDtypeStruct((ROWS, D), BF),
            jax.ShapeDtypeStruct((PAIRS, PART, 128), BF),
        ],
        scratch_shapes=scratch,
        compiler_params=pltpu.CompilerParams(
            vmem_limit_bytes=VMEM_LIMIT, collective_id=0, has_side_effects=True
        ),
    )(info, x, cot, wq, wk, wv, wo)


def assemble_kernel(att, gx, total, att_out, gx_out, gq, gk, gv, go):
    att_out[...] = att[...]
    gx_out[...] = gx[...]
    for p in range(3):
        at = slice(p * 128, p * 128 + 128)
        for n, ref in enumerate((gq, gk, gv)):
            ref[:, at] = total[p, n * D : n * D + D, :]
        for t in range(PAIRS):
            go[at, t * 128 : t * 128 + 128] = total[p, 3 * D + t * 128 : 3 * D + t * 128 + 128, :]


def assemble(att, gx, total):
    rows, square = jax.ShapeDtypeStruct((ROWS, D), BF), jax.ShapeDtypeStruct((D, D), BF)
    wide = pl.BlockSpec((ROWS // 2, D), lambda p: (p, 0))
    column = pl.BlockSpec((D, 384), lambda p: (0, p))
    return pl.pallas_call(
        assemble_kernel,
        grid=(2,),
        in_specs=[wide, wide, pl.BlockSpec((3, PART, 128), lambda p: (p, 0, 0))],
        out_specs=[wide, wide, column, column, column, pl.BlockSpec((384, D), lambda p: (p, 0))],
        out_shape=[rows, rows, square, square, square, square],
        compiler_params=pltpu.CompilerParams(vmem_limit_bytes=VMEM_LIMIT),
    )(att, gx, total)


def local(patches, wq, wk, wv, wo, lengths, cotangent):
    att, gx, total = sublayer(lengths, patches[0], cotangent[0], wq, wk, wv, wo)
    att, gx, *grads = assemble(att, gx, total)
    return (att[None], gx[None], *grads)


def solution(mesh):
    split = P("slide", "seq", None)
    return jax.shard_map(
        local,
        mesh=mesh,
        in_specs=(split, P(), P(), P(), P(), P("slide"), split),
        out_specs=(split, split, P(), P(), P(), P()),
        check_vma=False,
    )
```
